32 devices in a mesh: groups: 2 (over y), seq: 4 (over z), rep: 4 (over x, core).
Axes of the slice: x: 2, y: 2, z: 4, core: 2. Of those that a mesh axis runs over, the one named last changes fastest.
Arguments:
- hidden: bfloat16 [8, 512, 2048], P(('groups', 'rep'), 'seq'), parts along dimension 0, may hold values from -6 to 6
- shared_weight: bfloat16 [2048, 1024], P('seq'), may hold values from -0.125 to 0.125
- values: bfloat16 [8, 512, 1024], P(('groups', 'rep'), 'seq'), parts along dimension 0, may hold values from -6 to 6
- clusters: int32 [8, 512, 1], P(('groups', 'rep'), 'seq'), parts along dimension 0, may hold values from 0 to 7; in each aligned block of 128 rows (0 to 127, 128 to 255, ..., all dimensions but the last counted through in order) at most 32 rows name the same one
- cotangent: bfloat16 [8, 512, 1024], P(('groups', 'rep'), 'seq'), parts along dimension 0, may hold values from -6 to 6
Outputs:
- attended: bfloat16 [8, 512, 1024], P(('groups', 'rep'), 'seq'), parts along dimension 0
- hidden_grad: bfloat16 [8, 512, 2048], P(('groups', 'rep'), 'seq'), parts along dimension 0
- values_grad: bfloat16 [8, 512, 1024], P(('groups', 'rep'), 'seq'), parts along dimension 0
- weight_grad: float32 [4096, 1024], P(('groups', 'seq')), parts along dimension 0
The draws below stay inside these ranges and needn't reach their ends.
There are 2 independent parts, one for each index of `groups`. The reference program is written for one: setup_inputs(seed, part) draws one part's arguments, and reference() takes and returns one part's arrays. A program takes and returns all parts, laid end to end along the dimension named above; an argument that names none is the same for every part. Nothing has to cross between parts.
Inputs may be any that keep to these rules, and one draw needn't show every extreme that they name: `clusters`: within each aligned block of 128 tokens of a sequence, no cluster id occurs more than 32 times, and in every draw some id occurs exactly 32 times in some block.
All inputs are finite; a program needn't handle non-finite values.
Results may differ from the reference program's by a relative error of at most 0.014.
Values may be sent and summed in bfloat16 or wider, within the bound.
A program may use at most 64 MiB of HBM per device.

```python
import math
import jax
import jax.numpy as jnp
import numpy as np
from jax import lax

D = 2048
HEADS = 8
HEAD_SIZE = 128
TOK_DEV = 128
HD = 1024
CLUSTERS = 8
MOST = 32
CAPC = 128
LEN = 512
REPS = 4
N_SEQ = 4


def block_scale(own_key, shape, pieces, least, largest):
    loudness, own = 1.0, jax.random.fold_in(own_key, 6)
    for dim, blocks in pieces:
        steps = jnp.exp(jax.random.uniform(jax.random.fold_in(own, dim), (blocks,), jnp.float32, least / len(pieces), largest / len(pieces)))
        loudness = loudness * jnp.repeat(steps, shape[dim] // blocks).reshape([-1 if axis == dim else 1 for axis in range(len(shape))])
    return loudness


def deal_out(own_key, own, number, rows, count, top, most, lean):
    ranking = jax.random.permutation(own_key, count)
    heavy_load, common = portions_of(count, rows * top, most, lean, True), portions_of(count, rows * top, most, lean, False)
    places = jnp.arange(count)

    def named(lengths, turn):
        used = int((lengths > 0).sum())
        fixed = max(1, used // 4)
        shifted = fixed + (places - fixed + turn * (used - fixed)) % max(1, count - fixed)
        return jnp.zeros((count,), jnp.int32).at[ranking[jnp.where(places < fixed, places, shifted)]].set(jnp.asarray(lengths, jnp.int32))

    lengths = jnp.where(number % 4 == 0, named(heavy_load, number // 4), named(common, number - number // 4 - 1))
    mixed = jax.random.permutation(jax.random.fold_in(own, 3), count)
    giver, receiver = mixed[0:count // 2 * 2:2], mixed[1:count // 2 * 2:2]
    slack = jnp.minimum(lengths[giver] - 1, most - lengths[receiver]) // 2
    slack = jnp.where((giver == ranking[0]) | (receiver == ranking[0]) | (lengths[receiver] == 0), 0, jnp.maximum(slack, 0))
    shifted = jax.random.randint(jax.random.fold_in(own, 4), (count // 2,), 0, 1 << 20) % (slack + 1)
    lengths = lengths.at[giver].add(-shifted).at[receiver].add(shifted)
    labels = jnp.searchsorted(jnp.cumsum(lengths), jnp.arange(rows * top), side="right").astype(jnp.int32)
    table = labels.reshape(top, rows).T
    table = table[jax.random.permutation(jax.random.fold_in(own, 1), rows)]
    turn = jax.random.randint(jax.random.fold_in(own, 2), (rows, 1), 0, top)
    return jnp.take_along_axis(table, (jnp.arange(top)[None, :] + turn) % top, axis=1)


def portions_of(amount, total, reach, lean, full):
    weights = [(1 << 20) // math.isqrt(rank ** lean) + 1 for rank in range(1, amount + 1)]
    largest = reach if full else min(reach, max(-(-total // amount), total * weights[0] // sum(weights)))
    least = 1 if total - largest >= amount - 1 else 0
    given, spare = [largest] + [least] * (amount - 1), total - largest - least * (amount - 1)
    while spare > 0:
        free = [i for i in range(1, amount) if given[i] < largest] or [i for i in range(1, amount) if given[i] < reach]
        pool, budget = sum([weights[i] for i in free]), spare
        for i in free:
            more = min(reach - given[i], max(1, budget * weights[i] // pool), spare)
            given[i] = given[i] + more
            spare = spare - more
    return np.array(given)


def scatter_about(key, extent, deviation, bound, shards=(), kind=jnp.bfloat16):
    drawn = deviation * jax.random.normal(key, extent, jnp.float32)
    if shards:
        drawn = drawn * block_scale(key, extent, shards, -0.22, 0.18)
    return jnp.clip(drawn, -bound, bound).astype(kind)


def setup_inputs(seed: int = 0, part: int = 0) -> dict:
    key_of = jax.random.split(jax.random.key(seed), 6)
    own_keys = jax.random.split(jax.random.fold_in(key_of[5], part), 6)
    hidden = scatter_about(own_keys[0], (REPS, LEN, D), 1.0, 6.0, ((0, 4), (1, 4)))
    shared_weight = scatter_about(key_of[1], (D, HD), D ** -0.5, 0.125, ((0, 4),))
    values = scatter_about(own_keys[2], (REPS, LEN, HD), 1.0, 6.0, ((0, 4), (1, 4)))
    clusters_keys = jax.random.split(jax.random.fold_in(own_keys[3], 1), REPS * LEN // TOK_DEV)
    clusters_turns = jax.random.permutation(jax.random.fold_in(own_keys[3], 3), REPS * LEN // TOK_DEV)
    clusters = jax.vmap(lambda own, number: deal_out(jax.random.fold_in(own_keys[3], 2), own, number, TOK_DEV, CLUSTERS, 1, MOST, 2))(clusters_keys, clusters_turns).reshape((REPS, LEN, 1))
    cotangent = scatter_about(own_keys[4], (REPS, LEN, HD), 1.0, 6.0, ((0, 4), (1, 4)))
    return dict(hidden=hidden, shared_weight=shared_weight, values=values, clusters=clusters, cotangent=cotangent)


SOFTMAX_HEAT = 8.0
EPSILON = 1e-06

def cluster_step(q_rows, v_rows, g_rows, live):
    width = q_rows.shape[0]
    q3 = q_rows.astype(jnp.float32).reshape(width, HEADS, HEAD_SIZE)
    v3 = v_rows.astype(jnp.float32).reshape(width, HEADS, HEAD_SIZE)
    g3 = g_rows.astype(jnp.float32).reshape(width, HEADS, HEAD_SIZE)
    score_scale = SOFTMAX_HEAT / HEAD_SIZE
    index = jnp.arange(width, dtype=jnp.int32)
    before = (index[None, :] < index[:, None]) & live[:, None] & live[None, :]
    diagonal = index[None, :] == index[:, None]
    keep_mask = before | diagonal
    scores = jnp.einsum('ihd,jhd->hij', q3, q3) * score_scale
    score_logits = jnp.where(before[None], scores, 0.0)
    exponent_terms = jnp.where(keep_mask[None], jnp.exp(score_logits - SOFTMAX_HEAT), 0.0)
    probs = exponent_terms / lax.optimization_barrier(jnp.sum(exponent_terms, -1, keepdims=True))
    probs_low = probs.astype(jnp.bfloat16).astype(jnp.float32)
    attended = jnp.einsum('hij,jhd->ihd', probs_low, v3).astype(jnp.bfloat16)
    dprob = jnp.einsum('ihd,jhd->hij', g3, v3)
    delta = lax.optimization_barrier(jnp.sum(probs * dprob, -1, keepdims=True))
    dscore = jnp.where(before[None], probs * (dprob - delta), 0.0)
    dscore = dscore.astype(jnp.bfloat16).astype(jnp.float32)
    q_grad = score_scale * (jnp.einsum('hij,jhd->ihd', dscore, q3) + jnp.einsum('hji,jhd->ihd', dscore, q3))
    v_grad = jnp.einsum('hij,ihd->jhd', probs_low, g3)
    return (attended.reshape(width, HD), q_grad.astype(jnp.bfloat16).reshape(width, HD), v_grad.astype(jnp.bfloat16).reshape(width, HD))

def one_sequence(tokens, weight, value_rows, cluster_ids, grad_rows):
    projected = jnp.dot(tokens, weight, preferred_element_type=jnp.float32)
    grouped = projected.reshape(LEN, HEADS, HEAD_SIZE)
    inverse = lax.rsqrt(lax.optimization_barrier(jnp.mean(grouped * grouped, -1, keepdims=True)) + EPSILON)
    queries = (grouped * inverse).astype(jnp.bfloat16).reshape(LEN, HD)
    positions = jnp.arange(LEN, dtype=jnp.int32)
    order = jnp.argsort(cluster_ids * LEN + positions).astype(jnp.int32)
    counts = jax.ops.segment_sum(jnp.ones((LEN,), jnp.int32), cluster_ids, CLUSTERS)
    starts = jnp.cumsum(counts) - counts
    start_offsets = jnp.arange(CAPC, dtype=jnp.int32)
    window = jnp.clip(starts[:, None] + start_offsets[None, :], 0, LEN - 1)
    rows_index = order[window]
    live = start_offsets[None, :] < counts[:, None]

    def step(pair):
        picked, alive = pair
        return cluster_step(queries[picked], value_rows[picked], grad_rows[picked], alive)
    out_rows, q_rows, v_rows = lax.map(step, (rows_index, live))
    target = jnp.where(live, rows_index, LEN).reshape(-1)
    attended = jnp.zeros((LEN, HD), jnp.bfloat16).at[target].set(out_rows.reshape(-1, HD), mode='drop')
    q_grad = jnp.zeros((LEN, HD), jnp.bfloat16).at[target].set(q_rows.reshape(-1, HD), mode='drop')
    v_grad = jnp.zeros((LEN, HD), jnp.bfloat16).at[target].set(v_rows.reshape(-1, HD), mode='drop')
    dq = q_grad.astype(jnp.float32).reshape(LEN, HEADS, HEAD_SIZE)
    dy = inverse * dq - grouped * inverse ** 3 * lax.optimization_barrier(jnp.mean(dq * grouped, -1, keepdims=True))
    y_grad = dy.reshape(LEN, HD).astype(jnp.bfloat16)
    hidden_grad = jnp.dot(y_grad, weight.T, preferred_element_type=jnp.float32).astype(jnp.bfloat16)
    token_blocks = tokens.reshape(N_SEQ, TOK_DEV, D)
    grad_blocks = y_grad.reshape(N_SEQ, TOK_DEV, HD)

    def accumulate(total, pair):
        block_x, block_y = pair
        term = jnp.dot(block_x.T, block_y, preferred_element_type=jnp.float32).astype(jnp.bfloat16)
        term = lax.optimization_barrier(term)
        return (total + term.astype(jnp.float32), None)
    weight_grad, _ = lax.scan(accumulate, jnp.zeros((D, HD), jnp.float32), (token_blocks, grad_blocks))
    return (attended, hidden_grad, v_grad, weight_grad)

def reference(hidden, shared_weight, values, clusters, cotangent):
    outs_att = []
    outs_hid = []
    outs_val = []
    weight_grad = jnp.zeros((D, HD), jnp.float32)
    for seq_index in range(REPS):
        attended, hidden_grad, v_grad, w_term = one_sequence(hidden[seq_index], shared_weight, values[seq_index], clusters[seq_index, :, 0].astype(jnp.int32), cotangent[seq_index])
        outs_att.append(attended)
        outs_hid.append(hidden_grad)
        outs_val.append(v_grad)
        weight_grad = weight_grad + w_term
    return (jnp.stack(outs_att), jnp.stack(outs_hid), jnp.stack(outs_val), weight_grad)
```

```python
import jax
import jax.numpy as jnp
from jax import lax
from jax.experimental import pallas as pl
from jax.experimental.pallas import tpu as pltpu
from jax.sharding import PartitionSpec as P

HEADS = 8
HEAD_SIZE = 128
CL_DEV = 2


SOFTMAX_HEAT = 8.0
EPSILON = 1e-06


def attend_owned(received):
    q_recv, v_recv, g_recv, p_recv = received
    sources = q_recv.shape[0]
    items = q_recv.shape[1]
    slots = q_recv.shape[2]
    width = q_recv.shape[3]
    capacity = sources * slots

    def regroup(rows):
        return jnp.transpose(rows, (1, 0, 2, 3)).reshape(items, capacity, HEADS, HEAD_SIZE)

    query_four = regroup(q_recv)
    v_four = regroup(v_recv)
    g_four = regroup(g_recv)
    pos_items = jnp.transpose(p_recv, (1, 0, 2)).reshape(items, capacity)
    score_scale = SOFTMAX_HEAT / HEAD_SIZE
    scores = (
        jnp.einsum("nihd,njhd->nhij", query_four, query_four, preferred_element_type=jnp.float32)
        * score_scale
    )
    pos_row = pos_items[:, None, :, None]
    pos_col = pos_items[:, None, None, :]
    before = (pos_col < pos_row) & (pos_col >= 0)
    diagonal = jnp.eye(capacity, dtype=jnp.bool_)
    keep_mask = before | diagonal[None, None]
    score_logits = jnp.where(before, scores, 0.0)
    exponent_terms = jnp.where(keep_mask, jnp.exp(score_logits - SOFTMAX_HEAT), 0.0)
    probs = exponent_terms / jnp.sum(exponent_terms, -1, keepdims=True)
    probs_low = probs.astype(jnp.bfloat16)
    out_rows = jnp.einsum("nhij,njhd->nihd", probs_low, v_four, preferred_element_type=jnp.float32)
    dprob = jnp.einsum("nihd,njhd->nhij", g_four, v_four, preferred_element_type=jnp.float32)
    delta = jnp.sum(probs * dprob, -1, keepdims=True)
    dscore = jnp.where(before, probs * (dprob - delta), 0.0).astype(jnp.bfloat16)
    q_grad = score_scale * (
        jnp.einsum("nhij,njhd->nihd", dscore, query_four, preferred_element_type=jnp.float32)
        + jnp.einsum("nhji,njhd->nihd", dscore, query_four, preferred_element_type=jnp.float32)
    )
    v_grad = jnp.einsum("nhij,nihd->njhd", probs_low, g_four, preferred_element_type=jnp.float32)

    def restore(rows):
        shaped = rows.astype(jnp.bfloat16).reshape(items, sources, slots, width)
        return jnp.transpose(shaped, (1, 0, 2, 3))

    results = (restore(out_rows), restore(q_grad), restore(v_grad))
    return (
        lax.all_to_all(results[0], "seq", split_axis=0, concat_axis=0, tiled=True),
        lax.all_to_all(results[1], "seq", split_axis=0, concat_axis=0, tiled=True),
        lax.all_to_all(results[2], "seq", split_axis=0, concat_axis=0, tiled=True),
    )


def weight_rows(tokens, y_grad):
    summed = lax.psum_scatter(
        lax.dot_general(
            tokens, y_grad, (((0,), (0,)), ((), ())), preferred_element_type=jnp.float32
        ).astype(jnp.bfloat16),
        "seq",
        scatter_dimension=0,
        tiled=True,
    )
    return lax.psum(summed, "rep").astype(jnp.float32)


def input_grad(y_grad, weight_full):
    product = lax.dot_general(
        y_grad, weight_full, (((1,), (1,)), ((), ())), preferred_element_type=jnp.float32
    )
    return product.astype(jnp.bfloat16)


def local(hidden, shared_weight, values, clusters, cotangent):
    tokens = hidden[0]
    tok_count = tokens.shape[0]
    seq_count = lax.axis_size("seq")
    my_index = lax.axis_index("seq")
    n_clusters = CL_DEV * seq_count
    most = 2 * tok_count // n_clusters
    weight_full = lax.all_gather(shared_weight, "seq", axis=0, tiled=True)
    projected = jnp.dot(tokens, weight_full, preferred_element_type=jnp.float32)
    grouped = projected.reshape(tok_count, HEADS, HEAD_SIZE)
    inverse = lax.rsqrt(jnp.mean(grouped * grouped, -1, keepdims=True) + EPSILON)
    queries = (grouped * inverse).astype(jnp.bfloat16).reshape(tok_count, -1)
    width = queries.shape[1]
    cluster_ids = clusters[0, :, 0]
    one_hot = (cluster_ids[:, None] == jnp.arange(n_clusters, dtype=jnp.int32)[None, :]).astype(
        jnp.int32
    )
    rank = jnp.sum((jnp.cumsum(one_hot, 0) - one_hot) * one_hot, 1)
    slot = cluster_ids * most + rank
    n_slots = n_clusters * most

    def place(rows):
        filled = jnp.zeros((n_slots, width), jnp.bfloat16).at[slot].set(rows)
        return filled.reshape(seq_count, CL_DEV, most, width)

    positions = my_index * tok_count + jnp.arange(tok_count, dtype=jnp.int32)
    pos_send = (
        jnp.full((n_slots,), -1, jnp.int32).at[slot].set(positions).reshape(seq_count, CL_DEV, most)
    )
    back_att, back_q, back_v = attend_owned(
        (
            lax.all_to_all(place(queries), "seq", split_axis=0, concat_axis=0, tiled=True),
            lax.all_to_all(place(values[0]), "seq", split_axis=0, concat_axis=0, tiled=True),
            lax.all_to_all(place(cotangent[0]), "seq", split_axis=0, concat_axis=0, tiled=True),
            lax.all_to_all(pos_send, "seq", split_axis=0, concat_axis=0, tiled=True),
        )
    )
    attended = back_att.reshape(n_slots, width)[slot]
    q_tok = back_q.reshape(n_slots, width)[slot]
    v_tok = back_v.reshape(n_slots, width)[slot]
    dq = q_tok.astype(jnp.float32).reshape(tok_count, HEADS, HEAD_SIZE)
    dy = inverse * dq - grouped * inverse**3 * jnp.mean(dq * grouped, -1, keepdims=True)
    y_grad = dy.reshape(tok_count, width).astype(jnp.bfloat16)
    hidden_grad = input_grad(y_grad, weight_full)
    weight_grad = weight_rows(tokens, y_grad)
    return (attended[None], hidden_grad[None], v_tok[None], weight_grad)


SHIFTS = (1, 3, 2)
MESH = pl.DeviceIdType.MESH


def along_heads_kernel(
    hidden_ref, weight_ref, values_ref, cot_ref, cid_ref,
    att_ref, hg_ref, vg_ref, wg_ref,
    wbuf, vbuf, gbuf, pbuf, cbuf, hbuf, ybuf, hturn, qacc, vacc, acc,
    qbuf, sbuf_att, sbuf_vg, part, recv_core, both, recv_x,
    wsend, wrecv, csend, crecv, vsend, vrecv, gsend, grecv, psend, precv,
    hsend, hrecv, ysend, yrecv, asend, arecv, dsend, drecv, rsend, rrecv,
):
    n = 4
    z = lax.axis_index("seq")
    y = lax.axis_index("groups")
    rep = lax.axis_index("rep")
    x, core = rep // 2, rep % 2
    tok = hidden_ref.shape[0]
    depth = weight_ref.shape[0]
    wide = values_ref.shape[1] // n
    heads = wide // HEAD_SIZE
    scale = SOFTMAX_HEAT / HEAD_SIZE
    to_y = {"groups": 1 - y}
    to_x = {"rep": (1 - x) * 2 + core}
    to_core = {"rep": x * 2 + 1 - core}

    def to_seq(k):
        return {"seq": lax.rem(z + k, n)}

    def source(k):
        return lax.rem(z + n - k, n)

    def span(index, size):
        return pl.ds(pl.multiple_of(index * size, size), size)

    def remote(src, dst, send, recv, device):
        return pltpu.make_async_remote_copy(
            src_ref=src, dst_ref=dst, send_sem=send, recv_sem=recv,
            device_id=device, device_id_type=MESH,
        )

    barrier = pltpu.get_barrier_semaphore()
    for peer in [to_seq(k) for k in range(1, n)] + [to_y, to_x, to_core]:
        pl.semaphore_signal(barrier, inc=1, device_id=peer, device_id_type=MESH)
    pl.semaphore_wait(barrier, n + 2)

    started = []

    def start(copy):
        copy.start()
        started.append(copy)
        return copy

    half = depth // 2
    quarter = half // 2
    eighth = quarter // 2
    sixteenth = eighth // 2

    def rows_of(stage, part_half):
        a, b = (y, x) if part_half == 0 else (x, y)
        base = part_half * half + core * quarter
        if stage == 0:
            return pl.ds(pl.multiple_of(base + b * eighth + a * sixteenth, sixteenth), sixteenth)
        if stage == 1:
            return pl.ds(pl.multiple_of(base + b * eighth + a * sixteenth, sixteenth), sixteenth)
        if stage == 2:
            return pl.ds(pl.multiple_of(base + b * eighth, eighth), eighth)
        return pl.ds(pl.multiple_of(base, quarter), quarter)

    weight_copies = {}

    def weight_stage(stage, k, part_half):
        rows = rows_of(stage, part_half)
        if stage == 0:
            src, device = weight_ref.at[rows], to_seq(k)
        else:
            src = wbuf.at[k - 1, rows]
            first, second = (to_y, to_x) if part_half == 0 else (to_x, to_y)
            device = (first, second, to_core)[stage - 1]
        weight_copies[stage, k, part_half] = start(
            remote(
                src, wbuf.at[k - 1, rows],
                wsend.at[stage, k - 1, part_half], wrecv.at[stage, k - 1, part_half], device,
            )
        )

    cid_copies, v_copies, g_copies = {}, {}, {}
    for k in SHIFTS:
        for part_half in range(2):
            weight_stage(0, k, part_half)
    for k in SHIFTS:
        peer = lax.rem(z + k, n)
        cid_copies[k] = start(
            remote(cid_ref, cbuf.at[z], csend.at[k - 1], crecv.at[k - 1], to_seq(k))
        )
        v_copies[k] = start(
            remote(
                values_ref.at[:, span(peer, wide)], vbuf.at[span(z, tok)],
                vsend.at[k - 1], vrecv.at[k - 1], to_seq(k),
            )
        )
        g_copies[k] = start(
            remote(
                cot_ref.at[:, span(peer, wide)], gbuf.at[span(z, tok)],
                gsend.at[k - 1], grecv.at[k - 1], to_seq(k),
            )
        )
    vbuf[span(z, tok), :] = values_ref[:, span(z, wide)]
    gbuf[span(z, tok), :] = cot_ref[:, span(z, wide)]
    cbuf[z] = cid_ref[...]
    hbuf[span(z, tok), :] = hidden_ref[:, span(z, depth)]
    acc[...] = jnp.dot(
        hidden_ref[:, span(z, depth)], weight_ref[...], preferred_element_type=jnp.float32
    )

    for turn in range(len(SHIFTS) + 3):
        for stage in range(4):
            if 0 <= turn - stage < len(SHIFTS):
                k = SHIFTS[turn - stage]
                for part_half in range(2):
                    weight_copies[stage, k, part_half].wait_recv()
                    if stage < 3:
                        weight_stage(stage + 1, k, part_half)
                if stage == 3:
                    acc[...] += jnp.dot(
                        hidden_ref[:, span(source(k), depth)], wbuf[k - 1],
                        preferred_element_type=jnp.float32,
                    )

    for h in range(n):
        part[h, :tok, :] = acc[:, h * wide:(h + 1) * wide].astype(jnp.bfloat16)
    pbuf[span(z, tok), :] = part[z, :tok, :]
    p_copies, h_copies = {}, {}
    for k in SHIFTS:
        peer = lax.rem(z + k, n)
        p_copies[k] = start(
            remote(
                part.at[peer, pl.ds(0, tok)], pbuf.at[span(z, tok)],
                psend.at[k - 1], precv.at[k - 1], to_seq(k),
            )
        )
    for k in SHIFTS:
        peer = lax.rem(z + k, n)
        h_copies[k] = start(
            remote(
                hidden_ref.at[:, span(peer, depth)], hbuf.at[span(z, tok)],
                hsend.at[k - 1], hrecv.at[k - 1], to_seq(k),
            )
        )
    for k in SHIFTS:
        cid_copies[k].wait_recv()
        v_copies[k].wait_recv()
        g_copies[k].wait_recv()
    for k in SHIFTS:
        p_copies[k].wait_recv()
        p_copies[k].wait_send()

    id_rows = [cbuf[b] for b in range(n)]
    id_cols = [jnp.transpose(block)[:, 0:1] for block in id_rows]
    row_at = lax.broadcasted_iota(jnp.int32, (tok, tok), 0)
    col_at = lax.broadcasted_iota(jnp.int32, (tok, tok), 1)
    own = jnp.exp(jnp.float32(-SOFTMAX_HEAT))

    y_copies, a_copies, d_copies = {}, {}, {}
    nt = (((1,), (1,)), ((), ()))
    tn = (((0,), (0,)), ((), ()))
    for head in range(heads):
        cols = pl.ds(head * HEAD_SIZE, HEAD_SIZE)
        proj = pbuf[:, cols].astype(jnp.float32)
        inverse = lax.rsqrt(jnp.mean(proj * proj, -1, keepdims=True) + EPSILON)
        qbuf[head] = (proj * inverse).astype(jnp.bfloat16)
        qacc[...] = jnp.zeros_like(qacc)
        vacc[...] = jnp.zeros_like(vacc)
        for b in range(n):
            upto = (b + 1) * tok
            rows = pl.ds(b * tok, tok)
            q_b = qbuf[head, rows]
            g_b = gbuf[rows, cols]
            q_all = qbuf[head, pl.ds(0, upto)]
            v_all = vbuf[pl.ds(0, upto), cols]
            before = jnp.concatenate(
                [
                    (id_rows[j][0:1, :] == id_cols[b])
                    & ((col_at < row_at) if j == b else (col_at >= 0))
                    for j in range(b + 1)
                ],
                axis=1,
            )
            eye = (col_at == row_at) if b == 0 else jnp.concatenate(
                [jnp.zeros((tok, b * tok), jnp.float32), (col_at == row_at).astype(jnp.float32)],
                axis=1,
            ) > 0.5
            scores = lax.dot_general(q_b, q_all, nt, preferred_element_type=jnp.float32) * scale
            terms = jnp.where(
                before, jnp.exp(scores - SOFTMAX_HEAT), jnp.where(eye, own, 0.0)
            )
            probs = terms * (1.0 / jnp.sum(terms, -1, keepdims=True))
            low = probs.astype(jnp.bfloat16)
            sbuf_att[head, rows] = jnp.dot(
                low, v_all, preferred_element_type=jnp.float32
            ).astype(jnp.bfloat16)
            dprob = lax.dot_general(g_b, v_all, nt, preferred_element_type=jnp.float32)
            delta = jnp.sum(probs * dprob, -1, keepdims=True)
            dscore = jnp.where(before, probs * (dprob - delta), 0.0).astype(jnp.bfloat16)
            qacc[rows, :] += jnp.dot(dscore, q_all, preferred_element_type=jnp.float32)
            qacc[pl.ds(0, upto), :] += lax.dot_general(
                dscore, q_b, tn, preferred_element_type=jnp.float32
            )
            vacc[pl.ds(0, upto), :] += lax.dot_general(
                low, g_b, tn, preferred_element_type=jnp.float32
            )
        dq = (qacc[...] * scale).astype(jnp.bfloat16).astype(jnp.float32)
        dy = inverse * dq - proj * inverse**3 * jnp.mean(dq * proj, -1, keepdims=True)
        ybuf[0, :, cols] = dy.astype(jnp.bfloat16)
        sbuf_vg[head] = vacc[...].astype(jnp.bfloat16)
        for k in SHIFTS:
            y_copies[k, head] = start(
                remote(
                    ybuf.at[0, :, cols], ybuf.at[k, :, cols],
                    ysend.at[k - 1, head], yrecv.at[k - 1, head], to_seq(k),
                )
            )
        place = pl.ds(pl.multiple_of(z * wide + head * HEAD_SIZE, HEAD_SIZE), HEAD_SIZE)
        for k in SHIFTS:
            peer = lax.rem(z + k, n)
            a_copies[k, head] = start(
                remote(
                    sbuf_att.at[head, span(peer, tok)], att_ref.at[:, place],
                    asend.at[k - 1, head], arecv.at[k - 1, head], to_seq(k),
                )
            )
            d_copies[k, head] = start(
                remote(
                    sbuf_vg.at[head, span(peer, tok)], vg_ref.at[:, place],
                    dsend.at[k - 1, head], drecv.at[k - 1, head], to_seq(k),
                )
            )
        att_ref[:, place] = sbuf_att[head, span(z, tok)]
        vg_ref[:, place] = sbuf_vg[head, span(z, tok)]

    for k in SHIFTS:
        h_copies[k].wait_recv()
    hturn[...] = jnp.transpose(hbuf[...])

    mid = depth // 2
    mine = pl.ds(pl.multiple_of(core * mid, mid), mid)
    other = pl.ds(pl.multiple_of((1 - core) * mid, mid), mid)
    core_copies, x_copies, last_copies = {}, {}, {}

    def add_chips(k):
        x_copies[k].wait_recv()
        at = span(source(k), wide)
        total = both[k].astype(jnp.float32) + recv_x[k].astype(jnp.float32)
        wg_ref[mine, at] = total.astype(jnp.bfloat16)
        last_copies[k] = start(
            remote(
                wg_ref.at[mine, at], wg_ref.at[mine, at],
                rsend.at[2, k], rrecv.at[2, k], to_core,
            )
        )

    order = (0,) + SHIFTS
    for step, k in enumerate(order):
        if k > 0:
            for head in range(heads):
                y_copies[k, head].wait_recv()
        part[k] = jnp.dot(hturn[...], ybuf[k], preferred_element_type=jnp.float32).astype(
            jnp.bfloat16
        )
        core_copies[k] = start(
            remote(part.at[k, other], recv_core.at[k], rsend.at[0, k], rrecv.at[0, k], to_core)
        )
        if step >= 1:
            add_chips(order[step - 1])
        core_copies[k].wait_recv()
        both[k] = (
            part[k, mine, :].astype(jnp.float32) + recv_core[k].astype(jnp.float32)
        ).astype(jnp.bfloat16)
        x_copies[k] = start(
            remote(both.at[k], recv_x.at[k], rsend.at[1, k], rrecv.at[1, k], to_x)
        )

    own_rows = span(z, tok)
    for k in range(n):
        block = weight_ref if k == 0 else wbuf.at[k - 1]
        total = jnp.zeros((tok, depth), jnp.float32)
        for j in range(n):
            h = source(j)
            total = total + lax.dot_general(
                ybuf[j, own_rows, :], block[:, span(h, wide)], nt,
                preferred_element_type=jnp.float32,
            )
        hg_ref[:, span(source(k), depth)] = total.astype(jnp.bfloat16)
    add_chips(order[-1])

    for k in SHIFTS:
        for head in range(heads):
            a_copies[k, head].wait_recv()
            d_copies[k, head].wait_recv()
    for k in order:
        last_copies[k].wait_recv()
    done = set(id(copy) for copy in p_copies.values())
    for copy in started:
        if id(copy) not in done:
            copy.wait_send()


def local_by_heads(hidden, shared_weight, values, clusters, cotangent):
    n = 4
    tok, model = hidden.shape[1:]
    depth, width = shared_weight.shape
    wide = width // n
    length = n * tok
    heads = wide // HEAD_SIZE
    ids = jnp.broadcast_to(clusters[0, :, 0].astype(jnp.float32)[None, :], (8, tok))
    bf, f32 = jnp.bfloat16, jnp.float32
    vm = pltpu.VMEM
    dma = pltpu.SemaphoreType.DMA
    scratch = [
        vm((n - 1, depth, width), bf), vm((length, wide), bf), vm((length, wide), bf),
        vm((length, wide), bf), vm((n, 8, tok), f32), vm((length, depth), bf),
        vm((n, length, wide), bf), vm((depth, length), bf), vm((length, HEAD_SIZE), f32),
        vm((length, HEAD_SIZE), f32), vm((tok, width), f32),
        vm((heads, length, HEAD_SIZE), bf), vm((heads, length, HEAD_SIZE), bf),
        vm((heads, length, HEAD_SIZE), bf), vm((n, depth, wide), bf),
        vm((n, depth // 2, wide), bf), vm((n, depth // 2, wide), bf), vm((n, depth // 2, wide), bf),
        dma((4, n - 1, 2)), dma((4, n - 1, 2)),
    ]
    scratch += [dma((n - 1,)) for _ in range(10)]
    scratch += [dma((n - 1, heads)) for _ in range(6)]
    scratch += [dma((3, n)), dma((3, n))]
    att, hg, vg, wg = pl.pallas_call(
        along_heads_kernel,
        out_shape=(
            jax.ShapeDtypeStruct((tok, width), bf),
            jax.ShapeDtypeStruct((tok, model), bf),
            jax.ShapeDtypeStruct((tok, width), bf),
            jax.ShapeDtypeStruct((depth, width), bf),
        ),
        in_specs=[pl.BlockSpec(memory_space=pltpu.VMEM)] * 5,
        out_specs=[pl.BlockSpec(memory_space=pltpu.VMEM)] * 4,
        scratch_shapes=scratch,
        compiler_params=pltpu.CompilerParams(
            collective_id=0, has_side_effects=True, vmem_limit_bytes=48 * 1024 * 1024
        ),
        cost_estimate=pl.CostEstimate(
            flops=8 * tok * model * width, bytes_accessed=8 * 1024 * 1024, transcendentals=length * length
        ),
    )(hidden[0], shared_weight, values[0], cotangent[0], ids)
    return att[None], hg[None], vg[None], wg.astype(f32)


def solution(mesh):
    placed = (
        P(("groups", "rep"), "seq", None),
        P("seq", None),
        P(("groups", "rep"), "seq", None),
        P(("groups", "rep"), "seq", None),
        P(("groups", "rep"), "seq", None),
    )
    by_heads = (mesh.shape["groups"], mesh.shape["seq"], mesh.shape["rep"]) == (2, 4, 4)
    return jax.shard_map(
        local_by_heads if by_heads else local,
        mesh=mesh,
        in_specs=placed,
        out_specs=(
            P(("groups", "rep"), "seq", None),
            P(("groups", "rep"), "seq", None),
            P(("groups", "rep"), "seq", None),
            P(("groups", "seq"), None),
        ),
        check_vma=False,
    )
```

```python
import jax
import jax.numpy as jnp
from jax import lax
from jax.experimental import pallas as pl
from jax.experimental.pallas import tpu as pltpu
from jax.sharding import PartitionSpec as P

HEADS = 8
HEAD_SIZE = 128
CL_DEV = 2


SOFTMAX_HEAT = 8.0
EPSILON = 1e-06


def attend_owned(received):
    q_recv, v_recv, g_recv, p_recv = received
    sources = q_recv.shape[0]
    items = q_recv.shape[1]
    slots = q_recv.shape[2]
    width = q_recv.shape[3]
    capacity = sources * slots

    def regroup(rows):
        return jnp.transpose(rows, (1, 0, 2, 3)).reshape(items, capacity, HEADS, HEAD_SIZE)

    query_four = regroup(q_recv)
    v_four = regroup(v_recv)
    g_four = regroup(g_recv)
    pos_items = jnp.transpose(p_recv, (1, 0, 2)).reshape(items, capacity)
    score_scale = SOFTMAX_HEAT / HEAD_SIZE
    scores = (
        jnp.einsum("nihd,njhd->nhij", query_four, query_four, preferred_element_type=jnp.float32)
        * score_scale
    )
    pos_row = pos_items[:, None, :, None]
    pos_col = pos_items[:, None, None, :]
    before = (pos_col < pos_row) & (pos_col >= 0)
    diagonal = jnp.eye(capacity, dtype=jnp.bool_)
    keep_mask = before | diagonal[None, None]
    score_logits = jnp.where(before, scores, 0.0)
    exponent_terms = jnp.where(keep_mask, jnp.exp(score_logits - SOFTMAX_HEAT), 0.0)
    probs = exponent_terms / jnp.sum(exponent_terms, -1, keepdims=True)
    probs_low = probs.astype(jnp.bfloat16)
    out_rows = jnp.einsum("nhij,njhd->nihd", probs_low, v_four, preferred_element_type=jnp.float32)
    dprob = jnp.einsum("nihd,njhd->nhij", g_four, v_four, preferred_element_type=jnp.float32)
    delta = jnp.sum(probs * dprob, -1, keepdims=True)
    dscore = jnp.where(before, probs * (dprob - delta), 0.0).astype(jnp.bfloat16)
    q_grad = score_scale * (
        jnp.einsum("nhij,njhd->nihd", dscore, query_four, preferred_element_type=jnp.float32)
        + jnp.einsum("nhji,njhd->nihd", dscore, query_four, preferred_element_type=jnp.float32)
    )
    v_grad = jnp.einsum("nhij,nihd->njhd", probs_low, g_four, preferred_element_type=jnp.float32)

    def restore(rows):
        shaped = rows.astype(jnp.bfloat16).reshape(items, sources, slots, width)
        return jnp.transpose(shaped, (1, 0, 2, 3))

    results = (restore(out_rows), restore(q_grad), restore(v_grad))
    return (
        lax.all_to_all(results[0], "seq", split_axis=0, concat_axis=0, tiled=True),
        lax.all_to_all(results[1], "seq", split_axis=0, concat_axis=0, tiled=True),
        lax.all_to_all(results[2], "seq", split_axis=0, concat_axis=0, tiled=True),
    )


def weight_rows(tokens, y_grad):
    summed = lax.psum_scatter(
        lax.dot_general(
            tokens, y_grad, (((0,), (0,)), ((), ())), preferred_element_type=jnp.float32
        ).astype(jnp.bfloat16),
        "seq",
        scatter_dimension=0,
        tiled=True,
    )
    return lax.psum(summed, "rep").astype(jnp.float32)


def input_grad(y_grad, weight_full):
    product = lax.dot_general(
        y_grad, weight_full, (((1,), (1,)), ((), ())), preferred_element_type=jnp.float32
    )
    return product.astype(jnp.bfloat16)


def local(hidden, shared_weight, values, clusters, cotangent):
    tokens = hidden[0]
    tok_count = tokens.shape[0]
    seq_count = lax.axis_size("seq")
    my_index = lax.axis_index("seq")
    n_clusters = CL_DEV * seq_count
    most = 2 * tok_count // n_clusters
    weight_full = lax.all_gather(shared_weight, "seq", axis=0, tiled=True)
    projected = jnp.dot(tokens, weight_full, preferred_element_type=jnp.float32)
    grouped = projected.reshape(tok_count, HEADS, HEAD_SIZE)
    inverse = lax.rsqrt(jnp.mean(grouped * grouped, -1, keepdims=True) + EPSILON)
    queries = (grouped * inverse).astype(jnp.bfloat16).reshape(tok_count, -1)
    width = queries.shape[1]
    cluster_ids = clusters[0, :, 0]
    one_hot = (cluster_ids[:, None] == jnp.arange(n_clusters, dtype=jnp.int32)[None, :]).astype(
        jnp.int32
    )
    rank = jnp.sum((jnp.cumsum(one_hot, 0) - one_hot) * one_hot, 1)
    slot = cluster_ids * most + rank
    n_slots = n_clusters * most

    def place(rows):
        filled = jnp.zeros((n_slots, width), jnp.bfloat16).at[slot].set(rows)
        return filled.reshape(seq_count, CL_DEV, most, width)

    positions = my_index * tok_count + jnp.arange(tok_count, dtype=jnp.int32)
    pos_send = (
        jnp.full((n_slots,), -1, jnp.int32).at[slot].set(positions).reshape(seq_count, CL_DEV, most)
    )
    back_att, back_q, back_v = attend_owned(
        (
            lax.all_to_all(place(queries), "seq", split_axis=0, concat_axis=0, tiled=True),
            lax.all_to_all(place(values[0]), "seq", split_axis=0, concat_axis=0, tiled=True),
            lax.all_to_all(place(cotangent[0]), "seq", split_axis=0, concat_axis=0, tiled=True),
            lax.all_to_all(pos_send, "seq", split_axis=0, concat_axis=0, tiled=True),
        )
    )
    attended = back_att.reshape(n_slots, width)[slot]
    q_tok = back_q.reshape(n_slots, width)[slot]
    v_tok = back_v.reshape(n_slots, width)[slot]
    dq = q_tok.astype(jnp.float32).reshape(tok_count, HEADS, HEAD_SIZE)
    dy = inverse * dq - grouped * inverse**3 * jnp.mean(dq * grouped, -1, keepdims=True)
    y_grad = dy.reshape(tok_count, width).astype(jnp.bfloat16)
    hidden_grad = input_grad(y_grad, weight_full)
    weight_grad = weight_rows(tokens, y_grad)
    return (attended[None], hidden_grad[None], v_tok[None], weight_grad)


SHIFTS = (1, 3, 2)
MESH = pl.DeviceIdType.MESH


def along_heads_kernel(
    hidden_hbm, weight_hbm, values_hbm, cot_hbm, cid_ref,
    att_ref, hg_ref, vg_ref, wg_ref,
    hidden_ref, wbuf, vbuf, gbuf, pbuf, cbuf, hbuf, ybuf, hturn, qacc, vacc, acc,
    qbuf, sbuf_att, sbuf_vg, part, recv_core, both, recv_x,
    local_sem, zsend, zrecv, wsend, wrecv, csend, crecv, vsend, vrecv, gsend, grecv, psend, precv,
    hsend, hrecv, ysend, yrecv, asend, arecv, dsend, drecv, rsend, rrecv,
):
    n = 4
    z = lax.axis_index("seq")
    y = lax.axis_index("groups")
    rep = lax.axis_index("rep")
    x, core = rep // 2, rep % 2
    tok = hidden_ref.shape[0]
    depth = weight_hbm.shape[0]
    wide = values_hbm.shape[1] // n
    heads = wide // HEAD_SIZE
    scale = SOFTMAX_HEAT / HEAD_SIZE
    to_y = {"groups": 1 - y}
    to_x = {"rep": (1 - x) * 2 + core}
    to_core = {"rep": x * 2 + 1 - core}

    def to_seq(k):
        return {"seq": lax.rem(z + k, n)}

    inner = (z * (n - 1 - z)) > 0
    outward = {"seq": z + 1 - 2 * (z % 2)}
    across = {"seq": n - 1 - z}
    origins = (z, z + 1 - 2 * (z % 2), 2 - z // 2, 3 - 3 * (z // 2))

    def span(index, size):
        return pl.ds(pl.multiple_of(index * size, size), size)

    def remote(src, dst, send, recv, device):
        return pltpu.make_async_remote_copy(
            src_ref=src, dst_ref=dst, send_sem=send, recv_sem=recv,
            device_id=device, device_id_type=MESH,
        )

    loads = [
        pltpu.make_async_copy(src, dst, local_sem.at[index])
        for index, (src, dst) in enumerate(
            [
                (hidden_hbm, hidden_ref),
                (weight_hbm, wbuf.at[z]),
                (values_hbm.at[:, span(z, wide)], vbuf.at[span(z, tok)]),
                (cot_hbm.at[:, span(z, wide)], gbuf.at[span(z, tok)]),
                (hidden_hbm.at[:, span(z, depth)], hbuf.at[span(z, tok)]),
            ]
        )
    ]
    for load in loads:
        load.start()

    barrier = pltpu.get_barrier_semaphore()
    for peer in [to_seq(k) for k in range(1, n)] + [to_y, to_x, to_core]:
        pl.semaphore_signal(barrier, inc=1, device_id=peer, device_id_type=MESH)
    pl.semaphore_wait(barrier, n + 2)

    started, relayed = [], []

    def start(copy):
        copy.start()
        started.append(copy)
        return copy

    def relay(step, src, dst, send, recv):
        if step == 0:
            start(remote(src, dst, send.at[0], recv, outward))
        to_middle = step < 2
        copy = remote(
            src, dst, send.at[1 + step], recv, across if to_middle else outward
        )
        relayed.append(copy)

        @pl.when(inner)
        def _():
            copy.start()

    half = depth // 2
    quarter = half // 2
    eighth = quarter // 2
    sixteenth = eighth // 2

    def rows_of(stage, part_half):
        a, b = (y, x) if part_half == 0 else (x, y)
        base = part_half * half + core * quarter
        if stage == 0:
            return pl.ds(pl.multiple_of(base + b * eighth + a * sixteenth, sixteenth), sixteenth)
        if stage == 1:
            return pl.ds(pl.multiple_of(base + b * eighth + a * sixteenth, sixteenth), sixteenth)
        if stage == 2:
            return pl.ds(pl.multiple_of(base + b * eighth, eighth), eighth)
        return pl.ds(pl.multiple_of(base, quarter), quarter)

    weight_copies = {}

    def weight_relay(step, part_half):
        rows = rows_of(0, part_half)
        block = wbuf.at[origins[step], rows]
        relay(
            step, weight_hbm.at[rows] if step == 0 else block, block,
            zsend.at[part_half], zrecv.at[origins[step], part_half],
        )

    def weight_stage(stage, step, part_half):
        rows = rows_of(stage, part_half)
        block = wbuf.at[origins[step], rows]
        first, second = (to_y, to_x) if part_half == 0 else (to_x, to_y)
        weight_copies[stage, step, part_half] = start(
            remote(
                block, block,
                wsend.at[stage - 1, step - 1, part_half], wrecv.at[stage - 1, step - 1, part_half],
                (first, second, to_core)[stage - 1],
            )
        )

    cid_copies, v_copies, g_copies = {}, {}, {}
    for part_half in range(2):
        weight_relay(0, part_half)
    for k in SHIFTS:
        peer = lax.rem(z + k, n)
        cid_copies[k] = start(
            remote(cid_ref, cbuf.at[z], csend.at[k - 1], crecv.at[k - 1], to_seq(k))
        )
        v_copies[k] = start(
            remote(
                values_hbm.at[:, span(peer, wide)], vbuf.at[span(z, tok)],
                vsend.at[k - 1], vrecv.at[k - 1], to_seq(k),
            )
        )
        g_copies[k] = start(
            remote(
                cot_hbm.at[:, span(peer, wide)], gbuf.at[span(z, tok)],
                gsend.at[k - 1], grecv.at[k - 1], to_seq(k),
            )
        )
    cbuf[z] = cid_ref[...]
    for load in loads:
        load.wait()
    acc[...] = jnp.dot(
        hidden_ref[:, span(z, depth)], wbuf[z], preferred_element_type=jnp.float32
    )

    for turn in range(n + 2):
        for stage in range(n):
            step = turn - stage + 1
            if 1 <= step < n:
                for part_half in range(2):
                    if stage == 0:
                        block = wbuf.at[origins[step], rows_of(0, part_half)]
                        remote(
                            block, block, zsend.at[part_half, 0],
                            zrecv.at[origins[step], part_half], outward,
                        ).wait_recv()
                        weight_relay(step, part_half)
                    else:
                        weight_copies[stage, step, part_half].wait_recv()
                    if stage < 3:
                        weight_stage(stage + 1, step, part_half)
                if stage == 3:
                    acc[...] += jnp.dot(
                        hidden_ref[:, span(origins[step], depth)], wbuf[origins[step]],
                        preferred_element_type=jnp.float32,
                    )

    for h in range(n):
        part[h, :tok, :] = acc[:, h * wide:(h + 1) * wide].astype(jnp.bfloat16)
    pbuf[span(z, tok), :] = part[z, :tok, :]
    p_copies, h_copies = {}, {}
    for k in SHIFTS:
        peer = lax.rem(z + k, n)
        p_copies[k] = start(
            remote(
                part.at[peer, pl.ds(0, tok)], pbuf.at[span(z, tok)],
                psend.at[k - 1], precv.at[k - 1], to_seq(k),
            )
        )
    for k in SHIFTS:
        peer = lax.rem(z + k, n)
        h_copies[k] = start(
            remote(
                hidden_hbm.at[:, span(peer, depth)], hbuf.at[span(z, tok)],
                hsend.at[k - 1], hrecv.at[k - 1], to_seq(k),
            )
        )
    for k in SHIFTS:
        cid_copies[k].wait_recv()
        v_copies[k].wait_recv()
        g_copies[k].wait_recv()
    for k in SHIFTS:
        p_copies[k].wait_recv()
        p_copies[k].wait_send()

    id_rows = [cbuf[b] for b in range(n)]
    id_cols = [jnp.transpose(block)[:, 0:1] for block in id_rows]
    row_at = lax.broadcasted_iota(jnp.int32, (tok, tok), 0)
    col_at = lax.broadcasted_iota(jnp.int32, (tok, tok), 1)
    own = jnp.exp(jnp.float32(-SOFTMAX_HEAT))

    a_copies, d_copies = {}, {}

    def y_relay(step, head):
        block = ybuf.at[origins[step], :, pl.ds(head * HEAD_SIZE, HEAD_SIZE)]
        if step > 0:
            remote(
                block, block, ysend.at[head, 0], yrecv.at[origins[step], head], outward
            ).wait_recv()
        relay(step, block, block, ysend.at[head], yrecv.at[origins[step], head])

    def send_back():
        for head in range(heads):
            place = pl.ds(pl.multiple_of(z * wide + head * HEAD_SIZE, HEAD_SIZE), HEAD_SIZE)
            for k in SHIFTS:
                peer = lax.rem(z + k, n)
                a_copies[k, head] = start(
                    remote(
                        sbuf_att.at[head, span(peer, tok)], att_ref.at[:, place],
                        asend.at[k - 1, head], arecv.at[k - 1, head], to_seq(k),
                    )
                )
                d_copies[k, head] = start(
                    remote(
                        sbuf_vg.at[head, span(peer, tok)], vg_ref.at[:, place],
                        dsend.at[k - 1, head], drecv.at[k - 1, head], to_seq(k),
                    )
                )

    nt = (((1,), (1,)), ((), ()))
    tn = (((0,), (0,)), ((), ()))
    for head in range(heads):
        cols = pl.ds(head * HEAD_SIZE, HEAD_SIZE)
        proj = pbuf[:, cols].astype(jnp.float32)
        inverse = lax.rsqrt(jnp.mean(proj * proj, -1, keepdims=True) + EPSILON)
        qbuf[head] = (proj * inverse).astype(jnp.bfloat16)
        qacc[...] = jnp.zeros_like(qacc)
        vacc[...] = jnp.zeros_like(vacc)
        for b in range(n):
            upto = (b + 1) * tok
            rows = pl.ds(b * tok, tok)
            q_b = qbuf[head, rows]
            g_b = gbuf[rows, cols]
            q_all = qbuf[head, pl.ds(0, upto)]
            v_all = vbuf[pl.ds(0, upto), cols]
            before = jnp.concatenate(
                [
                    (id_rows[j][0:1, :] == id_cols[b])
                    & ((col_at < row_at) if j == b else (col_at >= 0))
                    for j in range(b + 1)
                ],
                axis=1,
            )
            eye = (col_at == row_at) if b == 0 else jnp.concatenate(
                [jnp.zeros((tok, b * tok), jnp.float32), (col_at == row_at).astype(jnp.float32)],
                axis=1,
            ) > 0.5
            scores = lax.dot_general(q_b, q_all, nt, preferred_element_type=jnp.float32) * scale
            terms = jnp.where(
                before, jnp.exp(scores - SOFTMAX_HEAT), jnp.where(eye, own, 0.0)
            )
            probs = terms * (1.0 / jnp.sum(terms, -1, keepdims=True))
            low = probs.astype(jnp.bfloat16)
            sbuf_att[head, rows] = jnp.dot(
                low, v_all, preferred_element_type=jnp.float32
            ).astype(jnp.bfloat16)
            dprob = lax.dot_general(g_b, v_all, nt, preferred_element_type=jnp.float32)
            delta = jnp.sum(probs * dprob, -1, keepdims=True)
            dscore = jnp.where(before, probs * (dprob - delta), 0.0).astype(jnp.bfloat16)
            qacc[rows, :] += jnp.dot(dscore, q_all, preferred_element_type=jnp.float32)
            qacc[pl.ds(0, upto), :] += lax.dot_general(
                dscore, q_b, tn, preferred_element_type=jnp.float32
            )
            vacc[pl.ds(0, upto), :] += lax.dot_general(
                low, g_b, tn, preferred_element_type=jnp.float32
            )
        dq = (qacc[...] * scale).astype(jnp.bfloat16).astype(jnp.float32)
        dy = inverse * dq - proj * inverse**3 * jnp.mean(dq * proj, -1, keepdims=True)
        ybuf[z, :, cols] = dy.astype(jnp.bfloat16)
        sbuf_vg[head] = vacc[...].astype(jnp.bfloat16)
        y_relay(0, head)
        place = pl.ds(pl.multiple_of(z * wide + head * HEAD_SIZE, HEAD_SIZE), HEAD_SIZE)
        att_ref[:, place] = sbuf_att[head, span(z, tok)]
        vg_ref[:, place] = sbuf_vg[head, span(z, tok)]

    for k in SHIFTS:
        h_copies[k].wait_recv()
    hturn[...] = jnp.transpose(hbuf[...])

    mid = depth // 2
    mine = pl.ds(pl.multiple_of(core * mid, mid), mid)
    other = pl.ds(pl.multiple_of((1 - core) * mid, mid), mid)
    core_copies, x_copies, last_copies = {}, {}, {}

    def add_chips(k):
        x_copies[k].wait_recv()
        at = span(origins[k], wide)
        total = both[k].astype(jnp.float32) + recv_x[k].astype(jnp.float32)
        wg_ref[mine, at] = total.astype(jnp.bfloat16)
        last_copies[k] = start(
            remote(
                wg_ref.at[mine, at], wg_ref.at[mine, at],
                rsend.at[2, k], rrecv.at[2, k], to_core,
            )
        )

    for k in range(n):
        if k > 0:
            for head in range(heads):
                y_relay(k, head)
        if k == 2:
            send_back()
        part[k] = jnp.dot(
            hturn[...], ybuf[origins[k]], preferred_element_type=jnp.float32
        ).astype(jnp.bfloat16)
        core_copies[k] = start(
            remote(part.at[k, other], recv_core.at[k], rsend.at[0, k], rrecv.at[0, k], to_core)
        )
        if k > 0:
            add_chips(k - 1)
        core_copies[k].wait_recv()
        both[k] = (
            part[k, mine, :].astype(jnp.float32) + recv_core[k].astype(jnp.float32)
        ).astype(jnp.bfloat16)
        x_copies[k] = start(
            remote(both.at[k], recv_x.at[k], rsend.at[1, k], rrecv.at[1, k], to_x)
        )

    own_rows = span(z, tok)
    for k in range(n):
        total = jnp.zeros((tok, depth), jnp.float32)
        for j in range(n):
            total = total + lax.dot_general(
                ybuf[origins[j], own_rows, :], wbuf[origins[k], :, span(origins[j], wide)], nt,
                preferred_element_type=jnp.float32,
            )
        hg_ref[:, span(origins[k], depth)] = total.astype(jnp.bfloat16)
    add_chips(n - 1)

    for k in SHIFTS:
        for head in range(heads):
            a_copies[k, head].wait_recv()
            d_copies[k, head].wait_recv()
    for k in range(n):
        last_copies[k].wait_recv()
    done = set(id(copy) for copy in p_copies.values())
    for copy in started:
        if id(copy) not in done:
            copy.wait_send()

    @pl.when(inner)
    def _():
        for copy in relayed:
            copy.wait_send()


def local_by_heads(hidden, shared_weight, values, clusters, cotangent):
    n = 4
    tok, model = hidden.shape[1:]
    depth, width = shared_weight.shape
    wide = width // n
    length = n * tok
    heads = wide // HEAD_SIZE
    ids = jnp.broadcast_to(clusters[0, :, 0].astype(jnp.float32)[None, :], (8, tok))
    bf, f32 = jnp.bfloat16, jnp.float32
    vm = pltpu.VMEM
    dma = pltpu.SemaphoreType.DMA
    scratch = [
        vm((tok, model), bf), vm((n, depth, width), bf), vm((length, wide), bf), vm((length, wide), bf),
        vm((length, wide), bf), vm((n, 8, tok), f32), vm((length, depth), bf),
        vm((n, length, wide), bf), vm((depth, length), bf), vm((length, HEAD_SIZE), f32),
        vm((length, HEAD_SIZE), f32), vm((tok, width), f32),
        vm((heads, length, HEAD_SIZE), bf), vm((heads, length, HEAD_SIZE), bf),
        vm((heads, length, HEAD_SIZE), bf), vm((n, depth, wide), bf),
        vm((n, depth // 2, wide), bf), vm((n, depth // 2, wide), bf), vm((n, depth // 2, wide), bf),
        dma((5,)), dma((2, n + 1)), dma((n, 2)), dma((3, n - 1, 2)), dma((3, n - 1, 2)),
    ]
    scratch += [dma((n - 1,)) for _ in range(10)]
    scratch += [dma((heads, n + 1)), dma((n, heads))]
    scratch += [dma((n - 1, heads)) for _ in range(4)]
    scratch += [dma((3, n)), dma((3, n))]
    att, hg, vg, wg = pl.pallas_call(
        along_heads_kernel,
        out_shape=(
            jax.ShapeDtypeStruct((tok, width), bf),
            jax.ShapeDtypeStruct((tok, model), bf),
            jax.ShapeDtypeStruct((tok, width), bf),
            jax.ShapeDtypeStruct((depth, width), bf),
        ),
        in_specs=[pl.BlockSpec(memory_space=pl.ANY)] * 4
        + [pl.BlockSpec(memory_space=pltpu.VMEM)],
        out_specs=[pl.BlockSpec(memory_space=pltpu.VMEM)] * 4,
        scratch_shapes=scratch,
        compiler_params=pltpu.CompilerParams(
            collective_id=0, has_side_effects=True, vmem_limit_bytes=48 * 1024 * 1024
        ),
        cost_estimate=pl.CostEstimate(
            flops=8 * tok * model * width, bytes_accessed=8 * 1024 * 1024, transcendentals=length * length
        ),
    )(hidden[0], shared_weight, values[0], cotangent[0], ids)
    return att[None], hg[None], vg[None], wg.astype(f32)


def solution(mesh):
    placed = (
        P(("groups", "rep"), "seq", None),
        P("seq", None),
        P(("groups", "rep"), "seq", None),
        P(("groups", "rep"), "seq", None),
        P(("groups", "rep"), "seq", None),
    )
    by_heads = (mesh.shape["groups"], mesh.shape["seq"], mesh.shape["rep"]) == (2, 4, 4)
    return jax.shard_map(
        local_by_heads if by_heads else local,
        mesh=mesh,
        in_specs=placed,
        out_specs=(
            P(("groups", "rep"), "seq", None),
            P(("groups", "rep"), "seq", None),
            P(("groups", "rep"), "seq", None),
            P(("groups", "seq"), None),
        ),
        check_vma=False,
    )
```

```python
import jax
import jax.numpy as jnp
from jax import lax
from jax.experimental import pallas as pl
from jax.experimental.pallas import tpu as pltpu
from jax.sharding import PartitionSpec as P

HEADS = 8
HEAD_SIZE = 128
CL_DEV = 2


SOFTMAX_HEAT = 8.0
EPSILON = 1e-06


def attend_owned(received):
    q_recv, v_recv, g_recv, p_recv = received
    sources = q_recv.shape[0]
    items = q_recv.shape[1]
    slots = q_recv.shape[2]
    width = q_recv.shape[3]
    capacity = sources * slots

    def regroup(rows):
        return jnp.transpose(rows, (1, 0, 2, 3)).reshape(items, capacity, HEADS, HEAD_SIZE)

    query_four = regroup(q_recv)
    v_four = regroup(v_recv)
    g_four = regroup(g_recv)
    pos_items = jnp.transpose(p_recv, (1, 0, 2)).reshape(items, capacity)
    score_scale = SOFTMAX_HEAT / HEAD_SIZE
    scores = (
        jnp.einsum("nihd,njhd->nhij", query_four, query_four, preferred_element_type=jnp.float32)
        * score_scale
    )
    pos_row = pos_items[:, None, :, None]
    pos_col = pos_items[:, None, None, :]
    before = (pos_col < pos_row) & (pos_col >= 0)
    diagonal = jnp.eye(capacity, dtype=jnp.bool_)
    keep_mask = before | diagonal[None, None]
    score_logits = jnp.where(before, scores, 0.0)
    exponent_terms = jnp.where(keep_mask, jnp.exp(score_logits - SOFTMAX_HEAT), 0.0)
    probs = exponent_terms / jnp.sum(exponent_terms, -1, keepdims=True)
    probs_low = probs.astype(jnp.bfloat16)
    out_rows = jnp.einsum("nhij,njhd->nihd", probs_low, v_four, preferred_element_type=jnp.float32)
    dprob = jnp.einsum("nihd,njhd->nhij", g_four, v_four, preferred_element_type=jnp.float32)
    delta = jnp.sum(probs * dprob, -1, keepdims=True)
    dscore = jnp.where(before, probs * (dprob - delta), 0.0).astype(jnp.bfloat16)
    q_grad = score_scale * (
        jnp.einsum("nhij,njhd->nihd", dscore, query_four, preferred_element_type=jnp.float32)
        + jnp.einsum("nhji,njhd->nihd", dscore, query_four, preferred_element_type=jnp.float32)
    )
    v_grad = jnp.einsum("nhij,nihd->njhd", probs_low, g_four, preferred_element_type=jnp.float32)

    def restore(rows):
        shaped = rows.astype(jnp.bfloat16).reshape(items, sources, slots, width)
        return jnp.transpose(shaped, (1, 0, 2, 3))

    results = (restore(out_rows), restore(q_grad), restore(v_grad))
    return (
        lax.all_to_all(results[0], "seq", split_axis=0, concat_axis=0, tiled=True),
        lax.all_to_all(results[1], "seq", split_axis=0, concat_axis=0, tiled=True),
        lax.all_to_all(results[2], "seq", split_axis=0, concat_axis=0, tiled=True),
    )


def weight_rows(tokens, y_grad):
    summed = lax.psum_scatter(
        lax.dot_general(
            tokens, y_grad, (((0,), (0,)), ((), ())), preferred_element_type=jnp.float32
        ).astype(jnp.bfloat16),
        "seq",
        scatter_dimension=0,
        tiled=True,
    )
    return lax.psum(summed, "rep").astype(jnp.float32)


def input_grad(y_grad, weight_full):
    product = lax.dot_general(
        y_grad, weight_full, (((1,), (1,)), ((), ())), preferred_element_type=jnp.float32
    )
    return product.astype(jnp.bfloat16)


def local(hidden, shared_weight, values, clusters, cotangent):
    tokens = hidden[0]
    tok_count = tokens.shape[0]
    seq_count = lax.axis_size("seq")
    my_index = lax.axis_index("seq")
    n_clusters = CL_DEV * seq_count
    most = 2 * tok_count // n_clusters
    weight_full = lax.all_gather(shared_weight, "seq", axis=0, tiled=True)
    projected = jnp.dot(tokens, weight_full, preferred_element_type=jnp.float32)
    grouped = projected.reshape(tok_count, HEADS, HEAD_SIZE)
    inverse = lax.rsqrt(jnp.mean(grouped * grouped, -1, keepdims=True) + EPSILON)
    queries = (grouped * inverse).astype(jnp.bfloat16).reshape(tok_count, -1)
    width = queries.shape[1]
    cluster_ids = clusters[0, :, 0]
    one_hot = (cluster_ids[:, None] == jnp.arange(n_clusters, dtype=jnp.int32)[None, :]).astype(
        jnp.int32
    )
    rank = jnp.sum((jnp.cumsum(one_hot, 0) - one_hot) * one_hot, 1)
    slot = cluster_ids * most + rank
    n_slots = n_clusters * most

    def place(rows):
        filled = jnp.zeros((n_slots, width), jnp.bfloat16).at[slot].set(rows)
        return filled.reshape(seq_count, CL_DEV, most, width)

    positions = my_index * tok_count + jnp.arange(tok_count, dtype=jnp.int32)
    pos_send = (
        jnp.full((n_slots,), -1, jnp.int32).at[slot].set(positions).reshape(seq_count, CL_DEV, most)
    )
    back_att, back_q, back_v = attend_owned(
        (
            lax.all_to_all(place(queries), "seq", split_axis=0, concat_axis=0, tiled=True),
            lax.all_to_all(place(values[0]), "seq", split_axis=0, concat_axis=0, tiled=True),
            lax.all_to_all(place(cotangent[0]), "seq", split_axis=0, concat_axis=0, tiled=True),
            lax.all_to_all(pos_send, "seq", split_axis=0, concat_axis=0, tiled=True),
        )
    )
    attended = back_att.reshape(n_slots, width)[slot]
    q_tok = back_q.reshape(n_slots, width)[slot]
    v_tok = back_v.reshape(n_slots, width)[slot]
    dq = q_tok.astype(jnp.float32).reshape(tok_count, HEADS, HEAD_SIZE)
    dy = inverse * dq - grouped * inverse**3 * jnp.mean(dq * grouped, -1, keepdims=True)
    y_grad = dy.reshape(tok_count, width).astype(jnp.bfloat16)
    hidden_grad = input_grad(y_grad, weight_full)
    weight_grad = weight_rows(tokens, y_grad)
    return (attended[None], hidden_grad[None], v_tok[None], weight_grad)


SHIFTS = (1, 3, 2)
MESH = pl.DeviceIdType.MESH


def along_heads_kernel(
    hidden_hbm, weight_hbm, values_hbm, cot_hbm, cid_ref,
    att_ref, hg_ref, vg_ref, wg_ref,
    hidden_ref, wbuf, vbuf, gbuf, pbuf, cbuf, hbuf, ybuf, hturn, qacc, vacc, acc,
    qbuf, sbuf_att, sbuf_vg, part, recv_core, both, recv_x,
    local_sem, zsend, zrecv, wsend, wrecv, csend, crecv, vsend, vrecv, gsend, grecv, psend, precv,
    hsend, hrecv, ysend, yrecv, asend, arecv, dsend, drecv, rsend, rrecv,
):
    n = 4
    z = lax.axis_index("seq")
    y = lax.axis_index("groups")
    rep = lax.axis_index("rep")
    x, core = rep // 2, rep % 2
    tok = hidden_ref.shape[0]
    depth = weight_hbm.shape[0]
    wide = values_hbm.shape[1] // n
    heads = wide // HEAD_SIZE
    scale = SOFTMAX_HEAT / HEAD_SIZE
    to_y = {"groups": 1 - y}
    to_x = {"rep": (1 - x) * 2 + core}
    to_core = {"rep": x * 2 + 1 - core}

    def to_seq(k):
        return {"seq": lax.rem(z + k, n)}

    inner = (z * (n - 1 - z)) > 0
    outward = {"seq": z + 1 - 2 * (z % 2)}
    across = {"seq": n - 1 - z}
    origins = (z, z + 1 - 2 * (z % 2), 2 - z // 2, 3 - 3 * (z // 2))

    def span(index, size):
        return pl.ds(pl.multiple_of(index * size, size), size)

    def remote(src, dst, send, recv, device):
        return pltpu.make_async_remote_copy(
            src_ref=src, dst_ref=dst, send_sem=send, recv_sem=recv,
            device_id=device, device_id_type=MESH,
        )

    loads = [
        pltpu.make_async_copy(src, dst, local_sem.at[index])
        for index, (src, dst) in enumerate(
            [
                (hidden_hbm, hidden_ref),
                (weight_hbm, wbuf.at[z]),
                (values_hbm.at[:, span(z, wide)], vbuf.at[span(z, tok)]),
                (cot_hbm.at[:, span(z, wide)], gbuf.at[span(z, tok)]),
                (hidden_hbm.at[:, span(z, depth)], hbuf.at[span(z, tok)]),
            ]
        )
    ]
    for load in loads:
        load.start()

    barrier = pltpu.get_barrier_semaphore()
    for peer in [to_seq(k) for k in range(1, n)] + [to_y, to_x, to_core]:
        pl.semaphore_signal(barrier, inc=1, device_id=peer, device_id_type=MESH)
    pl.semaphore_wait(barrier, n + 2)

    started, relayed = [], []

    def start(copy):
        copy.start()
        started.append(copy)
        return copy

    def relay(step, src, dst, send, recv):
        if step == 0:
            start(remote(src, dst, send.at[0], recv, outward))
        to_middle = step < 2
        copy = remote(
            src, dst, send.at[1 + step], recv, across if to_middle else outward
        )
        relayed.append(copy)

        @pl.when(inner)
        def _():
            copy.start()

    half = depth // 2
    quarter = half // 2
    eighth = quarter // 2
    sixteenth = eighth // 2

    def rows_of(stage, part_half):
        a, b = (y, x) if part_half == 0 else (x, y)
        base = part_half * half + core * quarter
        if stage == 0:
            return pl.ds(pl.multiple_of(base + b * eighth + a * sixteenth, sixteenth), sixteenth)
        if stage == 1:
            return pl.ds(pl.multiple_of(base + b * eighth + a * sixteenth, sixteenth), sixteenth)
        if stage == 2:
            return pl.ds(pl.multiple_of(base + b * eighth, eighth), eighth)
        return pl.ds(pl.multiple_of(base, quarter), quarter)

    weight_copies = {}

    def weight_relay(step, part_half):
        rows = rows_of(0, part_half)
        block = wbuf.at[origins[step], rows]
        relay(
            step, weight_hbm.at[rows] if step == 0 else block, block,
            zsend.at[part_half], zrecv.at[origins[step], part_half],
        )

    def weight_stage(stage, step, part_half):
        rows = rows_of(stage, part_half)
        block = wbuf.at[origins[step], rows]
        first, second = (to_y, to_x) if part_half == 0 else (to_x, to_y)
        weight_copies[stage, step, part_half] = start(
            remote(
                block, block,
                wsend.at[stage - 1, step - 1, part_half], wrecv.at[stage - 1, step - 1, part_half],
                (first, second, to_core)[stage - 1],
            )
        )

    cid_copies, v_copies, g_copies = {}, {}, {}
    for part_half in range(2):
        weight_relay(0, part_half)
    for k in SHIFTS:
        peer = lax.rem(z + k, n)
        cid_copies[k] = start(
            remote(cid_ref, cbuf.at[z], csend.at[k - 1], crecv.at[k - 1], to_seq(k))
        )

    def send_rows(kind, k):
        peer = lax.rem(z + k, n)
        src, dst, send, recv, kept = (
            (values_hbm, vbuf, vsend, vrecv, v_copies), (cot_hbm, gbuf, gsend, grecv, g_copies)
        )[kind]
        kept[k] = start(
            remote(
                src.at[:, span(peer, wide)], dst.at[span(z, tok)],
                send.at[k - 1], recv.at[k - 1], to_seq(k),
            )
        )

    waiting = [(kind, k) for kind in range(2) for k in SHIFTS]
    cbuf[z] = cid_ref[...]
    for load in loads:
        load.wait()
    acc[...] = jnp.dot(
        hidden_ref[:, span(z, depth)], wbuf[z], preferred_element_type=jnp.float32
    )

    for turn in range(n + 2):
        for stage in range(n):
            step = turn - stage + 1
            if 1 <= step < n:
                for part_half in range(2):
                    if stage == 0:
                        block = wbuf.at[origins[step], rows_of(0, part_half)]
                        remote(
                            block, block, zsend.at[part_half, 0],
                            zrecv.at[origins[step], part_half], outward,
                        ).wait_recv()
                        weight_relay(step, part_half)
                    else:
                        weight_copies[stage, step, part_half].wait_recv()
                    if stage < 3:
                        weight_stage(stage + 1, step, part_half)
                if stage == 3:
                    acc[...] += jnp.dot(
                        hidden_ref[:, span(origins[step], depth)], wbuf[origins[step]],
                        preferred_element_type=jnp.float32,
                    )
        if turn >= 2:
            for kind, k in waiting[2 * (turn - 2):2 * (turn - 1)]:
                send_rows(kind, k)

    for h in range(n):
        part[h, :tok, :] = acc[:, h * wide:(h + 1) * wide].astype(jnp.bfloat16)
    pbuf[span(z, tok), :] = part[z, :tok, :]
    p_copies, h_copies = {}, {}
    for k in SHIFTS:
        peer = lax.rem(z + k, n)
        p_copies[k] = start(
            remote(
                part.at[peer, pl.ds(0, tok)], pbuf.at[span(z, tok)],
                psend.at[k - 1], precv.at[k - 1], to_seq(k),
            )
        )
    for k in SHIFTS:
        peer = lax.rem(z + k, n)
        h_copies[k] = start(
            remote(
                hidden_hbm.at[:, span(peer, depth)], hbuf.at[span(z, tok)],
                hsend.at[k - 1], hrecv.at[k - 1], to_seq(k),
            )
        )
    for k in SHIFTS:
        cid_copies[k].wait_recv()
        v_copies[k].wait_recv()
        g_copies[k].wait_recv()
    for k in SHIFTS:
        p_copies[k].wait_recv()
        p_copies[k].wait_send()

    id_rows = [cbuf[b] for b in range(n)]
    id_cols = [jnp.transpose(block)[:, 0:1] for block in id_rows]
    row_at = lax.broadcasted_iota(jnp.int32, (tok, tok), 0)
    col_at = lax.broadcasted_iota(jnp.int32, (tok, tok), 1)
    own = jnp.exp(jnp.float32(-SOFTMAX_HEAT))

    a_copies, d_copies = {}, {}

    def y_relay(step, head):
        block = ybuf.at[origins[step], :, pl.ds(head * HEAD_SIZE, HEAD_SIZE)]
        if step > 0:
            remote(
                block, block, ysend.at[head, 0], yrecv.at[origins[step], head], outward
            ).wait_recv()
        relay(step, block, block, ysend.at[head], yrecv.at[origins[step], head])

    def send_back(which):
        for head in range(heads):
            place = pl.ds(pl.multiple_of(z * wide + head * HEAD_SIZE, HEAD_SIZE), HEAD_SIZE)
            for k in SHIFTS:
                peer = lax.rem(z + k, n)
                src, dst, send, recv, kept = (
                    (sbuf_att, att_ref, asend, arecv, a_copies),
                    (sbuf_vg, vg_ref, dsend, drecv, d_copies),
                )[which]
                kept[k, head] = start(
                    remote(
                        src.at[head, span(peer, tok)], dst.at[:, place],
                        send.at[k - 1, head], recv.at[k - 1, head], to_seq(k),
                    )
                )

    nt = (((1,), (1,)), ((), ()))
    tn = (((0,), (0,)), ((), ()))
    for head in range(heads):
        cols = pl.ds(head * HEAD_SIZE, HEAD_SIZE)
        proj = pbuf[:, cols].astype(jnp.float32)
        inverse = lax.rsqrt(jnp.mean(proj * proj, -1, keepdims=True) + EPSILON)
        qbuf[head] = (proj * inverse).astype(jnp.bfloat16)
        qacc[...] = jnp.zeros_like(qacc)
        vacc[...] = jnp.zeros_like(vacc)
        for b in range(n):
            upto = (b + 1) * tok
            rows = pl.ds(b * tok, tok)
            q_b = qbuf[head, rows]
            g_b = gbuf[rows, cols]
            q_all = qbuf[head, pl.ds(0, upto)]
            v_all = vbuf[pl.ds(0, upto), cols]
            before = jnp.concatenate(
                [
                    (id_rows[j][0:1, :] == id_cols[b])
                    & ((col_at < row_at) if j == b else (col_at >= 0))
                    for j in range(b + 1)
                ],
                axis=1,
            )
            eye = (col_at == row_at) if b == 0 else jnp.concatenate(
                [jnp.zeros((tok, b * tok), jnp.float32), (col_at == row_at).astype(jnp.float32)],
                axis=1,
            ) > 0.5
            scores = lax.dot_general(q_b, q_all, nt, preferred_element_type=jnp.float32) * scale
            terms = jnp.where(
                before, jnp.exp(scores - SOFTMAX_HEAT), jnp.where(eye, own, 0.0)
            )
            probs = terms * (1.0 / jnp.sum(terms, -1, keepdims=True))
            low = probs.astype(jnp.bfloat16)
            sbuf_att[head, rows] = jnp.dot(
                low, v_all, preferred_element_type=jnp.float32
            ).astype(jnp.bfloat16)
            dprob = lax.dot_general(g_b, v_all, nt, preferred_element_type=jnp.float32)
            delta = jnp.sum(probs * dprob, -1, keepdims=True)
            dscore = jnp.where(before, probs * (dprob - delta), 0.0).astype(jnp.bfloat16)
            qacc[rows, :] += jnp.dot(dscore, q_all, preferred_element_type=jnp.float32)
            qacc[pl.ds(0, upto), :] += lax.dot_general(
                dscore, q_b, tn, preferred_element_type=jnp.float32
            )
            vacc[pl.ds(0, upto), :] += lax.dot_general(
                low, g_b, tn, preferred_element_type=jnp.float32
            )
        dq = (qacc[...] * scale).astype(jnp.bfloat16).astype(jnp.float32)
        dy = inverse * dq - proj * inverse**3 * jnp.mean(dq * proj, -1, keepdims=True)
        ybuf[z, :, cols] = dy.astype(jnp.bfloat16)
        sbuf_vg[head] = vacc[...].astype(jnp.bfloat16)
        y_relay(0, head)
        place = pl.ds(pl.multiple_of(z * wide + head * HEAD_SIZE, HEAD_SIZE), HEAD_SIZE)
        att_ref[:, place] = sbuf_att[head, span(z, tok)]
        vg_ref[:, place] = sbuf_vg[head, span(z, tok)]

    for k in SHIFTS:
        h_copies[k].wait_recv()
    hturn[...] = jnp.transpose(hbuf[...])

    mid = depth // 2
    mine = pl.ds(pl.multiple_of(core * mid, mid), mid)
    other = pl.ds(pl.multiple_of((1 - core) * mid, mid), mid)
    core_copies, x_copies, last_copies = {}, {}, {}

    def add_chips(k):
        x_copies[k].wait_recv()
        at = span(origins[k], wide)
        total = both[k].astype(jnp.float32) + recv_x[k].astype(jnp.float32)
        wg_ref[mine, at] = total.astype(jnp.bfloat16)
        last_copies[k] = start(
            remote(
                wg_ref.at[mine, at], wg_ref.at[mine, at],
                rsend.at[2, k], rrecv.at[2, k], to_core,
            )
        )

    for k in range(n):
        if k > 0:
            for head in range(heads):
                y_relay(k, head)
        if k == 2:
            send_back(0)
        part[k] = jnp.dot(
            hturn[...], ybuf[origins[k]], preferred_element_type=jnp.float32
        ).astype(jnp.bfloat16)
        core_copies[k] = start(
            remote(part.at[k, other], recv_core.at[k], rsend.at[0, k], rrecv.at[0, k], to_core)
        )
        if k > 0:
            add_chips(k - 1)
        core_copies[k].wait_recv()
        both[k] = (
            part[k, mine, :].astype(jnp.float32) + recv_core[k].astype(jnp.float32)
        ).astype(jnp.bfloat16)
        x_copies[k] = start(
            remote(both.at[k], recv_x.at[k], rsend.at[1, k], rrecv.at[1, k], to_x)
        )

    send_back(1)
    own_rows = span(z, tok)
    for k in range(n):
        total = jnp.zeros((tok, depth), jnp.float32)
        for j in range(n):
            total = total + lax.dot_general(
                ybuf[origins[j], own_rows, :], wbuf[origins[k], :, span(origins[j], wide)], nt,
                preferred_element_type=jnp.float32,
            )
        hg_ref[:, span(origins[k], depth)] = total.astype(jnp.bfloat16)
    add_chips(n - 1)

    for k in SHIFTS:
        for head in range(heads):
            a_copies[k, head].wait_recv()
            d_copies[k, head].wait_recv()
    for k in range(n):
        last_copies[k].wait_recv()
    done = set(id(copy) for copy in p_copies.values())
    for copy in started:
        if id(copy) not in done:
            copy.wait_send()

    @pl.when(inner)
    def _():
        for copy in relayed:
            copy.wait_send()


def local_by_heads(hidden, shared_weight, values, clusters, cotangent):
    n = 4
    tok, model = hidden.shape[1:]
    depth, width = shared_weight.shape
    wide = width // n
    length = n * tok
    heads = wide // HEAD_SIZE
    ids = jnp.broadcast_to(clusters[0, :, 0].astype(jnp.float32)[None, :], (8, tok))
    bf, f32 = jnp.bfloat16, jnp.float32
    vm = pltpu.VMEM
    dma = pltpu.SemaphoreType.DMA
    scratch = [
        vm((tok, model), bf), vm((n, depth, width), bf), vm((length, wide), bf), vm((length, wide), bf),
        vm((length, wide), bf), vm((n, 8, tok), f32), vm((length, depth), bf),
        vm((n, length, wide), bf), vm((depth, length), bf), vm((length, HEAD_SIZE), f32),
        vm((length, HEAD_SIZE), f32), vm((tok, width), f32),
        vm((heads, length, HEAD_SIZE), bf), vm((heads, length, HEAD_SIZE), bf),
        vm((heads, length, HEAD_SIZE), bf), vm((n, depth, wide), bf),
        vm((n, depth // 2, wide), bf), vm((n, depth // 2, wide), bf), vm((n, depth // 2, wide), bf),
        dma((5,)), dma((2, n + 1)), dma((n, 2)), dma((3, n - 1, 2)), dma((3, n - 1, 2)),
    ]
    scratch += [dma((n - 1,)) for _ in range(10)]
    scratch += [dma((heads, n + 1)), dma((n, heads))]
    scratch += [dma((n - 1, heads)) for _ in range(4)]
    scratch += [dma((3, n)), dma((3, n))]
    att, hg, vg, wg = pl.pallas_call(
        along_heads_kernel,
        out_shape=(
            jax.ShapeDtypeStruct((tok, width), bf),
            jax.ShapeDtypeStruct((tok, model), bf),
            jax.ShapeDtypeStruct((tok, width), bf),
            jax.ShapeDtypeStruct((depth, width), bf),
        ),
        in_specs=[pl.BlockSpec(memory_space=pl.ANY)] * 4
        + [pl.BlockSpec(memory_space=pltpu.VMEM)],
        out_specs=[pl.BlockSpec(memory_space=pltpu.VMEM)] * 4,
        scratch_shapes=scratch,
        compiler_params=pltpu.CompilerParams(
            collective_id=0, has_side_effects=True, vmem_limit_bytes=48 * 1024 * 1024
        ),
        cost_estimate=pl.CostEstimate(
            flops=8 * tok * model * width, bytes_accessed=8 * 1024 * 1024, transcendentals=length * length
        ),
    )(hidden[0], shared_weight, values[0], cotangent[0], ids)
    return att[None], hg[None], vg[None], wg.astype(f32)


def solution(mesh):
    placed = (
        P(("groups", "rep"), "seq", None),
        P("seq", None),
        P(("groups", "rep"), "seq", None),
        P(("groups", "rep"), "seq", None),
        P(("groups", "rep"), "seq", None),
    )
    by_heads = (mesh.shape["groups"], mesh.shape["seq"], mesh.shape["rep"]) == (2, 4, 4)
    return jax.shard_map(
        local_by_heads if by_heads else local,
        mesh=mesh,
        in_specs=placed,
        out_specs=(
            P(("groups", "rep"), "seq", None),
            P(("groups", "rep"), "seq", None),
            P(("groups", "rep"), "seq", None),
            P(("groups", "seq"), None),
        ),
        check_vma=False,
    )
```

```python
import jax
import jax.numpy as jnp
from jax import lax
from jax.experimental import pallas as pl
from jax.experimental.pallas import tpu as pltpu
from jax.sharding import PartitionSpec as P

HEADS = 8
HEAD_SIZE = 128
CL_DEV = 2


SOFTMAX_HEAT = 8.0
EPSILON = 1e-06


def attend_owned(received):
    q_recv, v_recv, g_recv, p_recv = received
    sources = q_recv.shape[0]
    items = q_recv.shape[1]
    slots = q_recv.shape[2]
    width = q_recv.shape[3]
    capacity = sources * slots

    def regroup(rows):
        return jnp.transpose(rows, (1, 0, 2, 3)).reshape(items, capacity, HEADS, HEAD_SIZE)

    query_four = regroup(q_recv)
    v_four = regroup(v_recv)
    g_four = regroup(g_recv)
    pos_items = jnp.transpose(p_recv, (1, 0, 2)).reshape(items, capacity)
    score_scale = SOFTMAX_HEAT / HEAD_SIZE
    scores = (
        jnp.einsum("nihd,njhd->nhij", query_four, query_four, preferred_element_type=jnp.float32)
        * score_scale
    )
    pos_row = pos_items[:, None, :, None]
    pos_col = pos_items[:, None, None, :]
    before = (pos_col < pos_row) & (pos_col >= 0)
    diagonal = jnp.eye(capacity, dtype=jnp.bool_)
    keep_mask = before | diagonal[None, None]
    score_logits = jnp.where(before, scores, 0.0)
    exponent_terms = jnp.where(keep_mask, jnp.exp(score_logits - SOFTMAX_HEAT), 0.0)
    probs = exponent_terms / jnp.sum(exponent_terms, -1, keepdims=True)
    probs_low = probs.astype(jnp.bfloat16)
    out_rows = jnp.einsum("nhij,njhd->nihd", probs_low, v_four, preferred_element_type=jnp.float32)
    dprob = jnp.einsum("nihd,njhd->nhij", g_four, v_four, preferred_element_type=jnp.float32)
    delta = jnp.sum(probs * dprob, -1, keepdims=True)
    dscore = jnp.where(before, probs * (dprob - delta), 0.0).astype(jnp.bfloat16)
    q_grad = score_scale * (
        jnp.einsum("nhij,njhd->nihd", dscore, query_four, preferred_element_type=jnp.float32)
        + jnp.einsum("nhji,njhd->nihd", dscore, query_four, preferred_element_type=jnp.float32)
    )
    v_grad = jnp.einsum("nhij,nihd->njhd", probs_low, g_four, preferred_element_type=jnp.float32)

    def restore(rows):
        shaped = rows.astype(jnp.bfloat16).reshape(items, sources, slots, width)
        return jnp.transpose(shaped, (1, 0, 2, 3))

    results = (restore(out_rows), restore(q_grad), restore(v_grad))
    return (
        lax.all_to_all(results[0], "seq", split_axis=0, concat_axis=0, tiled=True),
        lax.all_to_all(results[1], "seq", split_axis=0, concat_axis=0, tiled=True),
        lax.all_to_all(results[2], "seq", split_axis=0, concat_axis=0, tiled=True),
    )


def weight_rows(tokens, y_grad):
    summed = lax.psum_scatter(
        lax.dot_general(
            tokens, y_grad, (((0,), (0,)), ((), ())), preferred_element_type=jnp.float32
        ).astype(jnp.bfloat16),
        "seq",
        scatter_dimension=0,
        tiled=True,
    )
    return lax.psum(summed, "rep").astype(jnp.float32)


def input_grad(y_grad, weight_full):
    product = lax.dot_general(
        y_grad, weight_full, (((1,), (1,)), ((), ())), preferred_element_type=jnp.float32
    )
    return product.astype(jnp.bfloat16)


def local(hidden, shared_weight, values, clusters, cotangent):
    tokens = hidden[0]
    tok_count = tokens.shape[0]
    seq_count = lax.axis_size("seq")
    my_index = lax.axis_index("seq")
    n_clusters = CL_DEV * seq_count
    most = 2 * tok_count // n_clusters
    weight_full = lax.all_gather(shared_weight, "seq", axis=0, tiled=True)
    projected = jnp.dot(tokens, weight_full, preferred_element_type=jnp.float32)
    grouped = projected.reshape(tok_count, HEADS, HEAD_SIZE)
    inverse = lax.rsqrt(jnp.mean(grouped * grouped, -1, keepdims=True) + EPSILON)
    queries = (grouped * inverse).astype(jnp.bfloat16).reshape(tok_count, -1)
    width = queries.shape[1]
    cluster_ids = clusters[0, :, 0]
    one_hot = (cluster_ids[:, None] == jnp.arange(n_clusters, dtype=jnp.int32)[None, :]).astype(
        jnp.int32
    )
    rank = jnp.sum((jnp.cumsum(one_hot, 0) - one_hot) * one_hot, 1)
    slot = cluster_ids * most + rank
    n_slots = n_clusters * most

    def place(rows):
        filled = jnp.zeros((n_slots, width), jnp.bfloat16).at[slot].set(rows)
        return filled.reshape(seq_count, CL_DEV, most, width)

    positions = my_index * tok_count + jnp.arange(tok_count, dtype=jnp.int32)
    pos_send = (
        jnp.full((n_slots,), -1, jnp.int32).at[slot].set(positions).reshape(seq_count, CL_DEV, most)
    )
    back_att, back_q, back_v = attend_owned(
        (
            lax.all_to_all(place(queries), "seq", split_axis=0, concat_axis=0, tiled=True),
            lax.all_to_all(place(values[0]), "seq", split_axis=0, concat_axis=0, tiled=True),
            lax.all_to_all(place(cotangent[0]), "seq", split_axis=0, concat_axis=0, tiled=True),
            lax.all_to_all(pos_send, "seq", split_axis=0, concat_axis=0, tiled=True),
        )
    )
    attended = back_att.reshape(n_slots, width)[slot]
    q_tok = back_q.reshape(n_slots, width)[slot]
    v_tok = back_v.reshape(n_slots, width)[slot]
    dq = q_tok.astype(jnp.float32).reshape(tok_count, HEADS, HEAD_SIZE)
    dy = inverse * dq - grouped * inverse**3 * jnp.mean(dq * grouped, -1, keepdims=True)
    y_grad = dy.reshape(tok_count, width).astype(jnp.bfloat16)
    hidden_grad = input_grad(y_grad, weight_full)
    weight_grad = weight_rows(tokens, y_grad)
    return (attended[None], hidden_grad[None], v_tok[None], weight_grad)


SHIFTS = (1, 3, 2)
MESH = pl.DeviceIdType.MESH


def along_heads_kernel(
    hidden_hbm, weight_hbm, values_hbm, cot_hbm, cid_ref,
    att_ref, hg_ref, vg_ref, wg_ref,
    hidden_ref, wbuf, vbuf, gbuf, pbuf, cbuf, hbuf, ybuf, hturn, qacc, vacc, acc,
    qbuf, sbuf_att, sbuf_vg, part, recv_core, both, recv_x,
    local_sem, zsend, zrecv, wsend, wrecv, csend, crecv, vsend, vrecv, gsend, grecv, psend, precv,
    hsend, hrecv, ysend, yrecv, asend, arecv, dsend, drecv, rsend, rrecv,
):
    n = 4
    z = lax.axis_index("seq")
    y = lax.axis_index("groups")
    rep = lax.axis_index("rep")
    x, core = rep // 2, rep % 2
    tok = hidden_ref.shape[0]
    depth = weight_hbm.shape[0]
    wide = values_hbm.shape[1] // n
    heads = wide // HEAD_SIZE
    scale = SOFTMAX_HEAT / HEAD_SIZE
    to_y = {"groups": 1 - y}
    to_x = {"rep": (1 - x) * 2 + core}
    to_core = {"rep": x * 2 + 1 - core}

    def to_seq(k):
        return {"seq": lax.rem(z + k, n)}

    inner = (z * (n - 1 - z)) > 0
    outward = {"seq": z + 1 - 2 * (z % 2)}
    across = {"seq": n - 1 - z}
    origins = (z, z + 1 - 2 * (z % 2), 2 - z // 2, 3 - 3 * (z // 2))

    def span(index, size):
        return pl.ds(pl.multiple_of(index * size, size), size)

    def remote(src, dst, send, recv, device):
        return pltpu.make_async_remote_copy(
            src_ref=src, dst_ref=dst, send_sem=send, recv_sem=recv,
            device_id=device, device_id_type=MESH,
        )

    loads = [
        pltpu.make_async_copy(src, dst, local_sem.at[index])
        for index, (src, dst) in enumerate(
            [
                (hidden_hbm, hidden_ref),
                (weight_hbm, wbuf.at[z]),
                (values_hbm.at[:, span(z, wide)], vbuf.at[span(z, tok)]),
                (cot_hbm.at[:, span(z, wide)], gbuf.at[span(z, tok)]),
                (hidden_hbm.at[:, span(z, depth)], hbuf.at[span(z, tok)]),
            ]
        )
    ]
    for load in loads:
        load.start()

    barrier = pltpu.get_barrier_semaphore()
    for peer in [to_seq(k) for k in range(1, n)] + [to_y, to_x, to_core]:
        pl.semaphore_signal(barrier, inc=1, device_id=peer, device_id_type=MESH)
    pl.semaphore_wait(barrier, n + 2)

    started, relayed = [], []

    def start(copy):
        copy.start()
        started.append(copy)
        return copy

    def relay(step, src, dst, send, recv):
        if step == 0:
            start(remote(src, dst, send.at[0], recv, outward))
        to_middle = step < 2
        copy = remote(
            src, dst, send.at[1 + step], recv, across if to_middle else outward
        )
        relayed.append(copy)

        @pl.when(inner)
        def _():
            copy.start()

    half = depth // 2
    quarter = half // 2
    eighth = quarter // 2
    sixteenth = eighth // 2

    def rows_of(stage, part_half):
        a, b = (y, x) if part_half == 0 else (x, y)
        base = part_half * half + core * quarter
        if stage == 0:
            return pl.ds(pl.multiple_of(base + b * eighth + a * sixteenth, sixteenth), sixteenth)
        if stage == 1:
            return pl.ds(pl.multiple_of(base + b * eighth + a * sixteenth, sixteenth), sixteenth)
        if stage == 2:
            return pl.ds(pl.multiple_of(base + b * eighth, eighth), eighth)
        return pl.ds(pl.multiple_of(base, quarter), quarter)

    weight_copies = {}

    def weight_relay(step, part_half):
        rows = rows_of(0, part_half)
        block = wbuf.at[origins[step], rows]
        relay(
            step, weight_hbm.at[rows] if step == 0 else block, block,
            zsend.at[part_half], zrecv.at[origins[step], part_half],
        )

    def weight_stage(stage, step, part_half):
        rows = rows_of(stage, part_half)
        block = wbuf.at[origins[step], rows]
        first, second = (to_y, to_x) if part_half == 0 else (to_x, to_y)
        weight_copies[stage, step, part_half] = start(
            remote(
                block, block,
                wsend.at[stage - 1, step - 1, part_half], wrecv.at[stage - 1, step - 1, part_half],
                (first, second, to_core)[stage - 1],
            )
        )

    cid_copies, v_copies, g_copies = {}, {}, {}
    for part_half in range(2):
        weight_relay(0, part_half)
    for k in SHIFTS:
        peer = lax.rem(z + k, n)
        cid_copies[k] = start(
            remote(cid_ref, cbuf.at[z], csend.at[k - 1], crecv.at[k - 1], to_seq(k))
        )

    def send_rows(kind, k):
        peer = lax.rem(z + k, n)
        src, dst, send, recv, kept = (
            (values_hbm, vbuf, vsend, vrecv, v_copies), (cot_hbm, gbuf, gsend, grecv, g_copies)
        )[kind]
        kept[k] = start(
            remote(
                src.at[:, span(peer, wide)], dst.at[span(z, tok)],
                send.at[k - 1], recv.at[k - 1], to_seq(k),
            )
        )

    waiting = [(kind, k) for kind in range(2) for k in SHIFTS]
    cbuf[z] = cid_ref[...]
    for load in loads:
        load.wait()
    acc[...] = jnp.dot(
        hidden_ref[:, span(z, depth)], wbuf[z], preferred_element_type=jnp.float32
    )

    for turn in range(n + 2):
        for stage in range(n):
            step = turn - stage + 1
            if 1 <= step < n:
                for part_half in range(2):
                    if stage == 0:
                        block = wbuf.at[origins[step], rows_of(0, part_half)]
                        remote(
                            block, block, zsend.at[part_half, 0],
                            zrecv.at[origins[step], part_half], outward,
                        ).wait_recv()
                        weight_relay(step, part_half)
                    else:
                        weight_copies[stage, step, part_half].wait_recv()
                    if stage < 3:
                        weight_stage(stage + 1, step, part_half)
                if stage == 3:
                    acc[...] += jnp.dot(
                        hidden_ref[:, span(origins[step], depth)], wbuf[origins[step]],
                        preferred_element_type=jnp.float32,
                    )
        if turn >= 2:
            for kind, k in waiting[3 * (turn - 2):3 * (turn - 1)]:
                send_rows(kind, k)

    for h in range(n):
        part[h, :tok, :] = acc[:, h * wide:(h + 1) * wide].astype(jnp.bfloat16)
    pbuf[span(z, tok), :] = part[z, :tok, :]
    p_copies, h_copies = {}, {}
    for k in SHIFTS:
        peer = lax.rem(z + k, n)
        p_copies[k] = start(
            remote(
                part.at[peer, pl.ds(0, tok)], pbuf.at[span(z, tok)],
                psend.at[k - 1], precv.at[k - 1], to_seq(k),
            )
        )
    for k in SHIFTS:
        peer = lax.rem(z + k, n)
        h_copies[k] = start(
            remote(
                hidden_hbm.at[:, span(peer, depth)], hbuf.at[span(z, tok)],
                hsend.at[k - 1], hrecv.at[k - 1], to_seq(k),
            )
        )
    for k in SHIFTS:
        cid_copies[k].wait_recv()
        v_copies[k].wait_recv()
        g_copies[k].wait_recv()
    for k in SHIFTS:
        p_copies[k].wait_recv()
        p_copies[k].wait_send()

    id_rows = [cbuf[b] for b in range(n)]
    id_cols = [jnp.transpose(block)[:, 0:1] for block in id_rows]
    row_at = lax.broadcasted_iota(jnp.int32, (tok, tok), 0)
    col_at = lax.broadcasted_iota(jnp.int32, (tok, tok), 1)
    own = jnp.exp(jnp.float32(-SOFTMAX_HEAT))

    a_copies, d_copies = {}, {}

    def y_relay(step, head):
        block = ybuf.at[origins[step], :, pl.ds(head * HEAD_SIZE, HEAD_SIZE)]
        if step > 0:
            remote(
                block, block, ysend.at[head, 0], yrecv.at[origins[step], head], outward
            ).wait_recv()
        relay(step, block, block, ysend.at[head], yrecv.at[origins[step], head])

    def send_back(which):
        for head in range(heads):
            place = pl.ds(pl.multiple_of(z * wide + head * HEAD_SIZE, HEAD_SIZE), HEAD_SIZE)
            for k in SHIFTS:
                peer = lax.rem(z + k, n)
                src, dst, send, recv, kept = (
                    (sbuf_att, att_ref, asend, arecv, a_copies),
                    (sbuf_vg, vg_ref, dsend, drecv, d_copies),
                )[which]
                kept[k, head] = start(
                    remote(
                        src.at[head, span(peer, tok)], dst.at[:, place],
                        send.at[k - 1, head], recv.at[k - 1, head], to_seq(k),
                    )
                )

    nt = (((1,), (1,)), ((), ()))
    tn = (((0,), (0,)), ((), ()))
    for head in range(heads):
        cols = pl.ds(head * HEAD_SIZE, HEAD_SIZE)
        proj = pbuf[:, cols].astype(jnp.float32)
        inverse = lax.rsqrt(jnp.mean(proj * proj, -1, keepdims=True) + EPSILON)
        qbuf[head] = (proj * inverse).astype(jnp.bfloat16)
        qacc[...] = jnp.zeros_like(qacc)
        vacc[...] = jnp.zeros_like(vacc)
        for b in range(n):
            upto = (b + 1) * tok
            rows = pl.ds(b * tok, tok)
            q_b = qbuf[head, rows]
            g_b = gbuf[rows, cols]
            q_all = qbuf[head, pl.ds(0, upto)]
            v_all = vbuf[pl.ds(0, upto), cols]
            before = jnp.concatenate(
                [
                    (id_rows[j][0:1, :] == id_cols[b])
                    & ((col_at < row_at) if j == b else (col_at >= 0))
                    for j in range(b + 1)
                ],
                axis=1,
            )
            eye = (col_at == row_at) if b == 0 else jnp.concatenate(
                [jnp.zeros((tok, b * tok), jnp.float32), (col_at == row_at).astype(jnp.float32)],
                axis=1,
            ) > 0.5
            scores = lax.dot_general(q_b, q_all, nt, preferred_element_type=jnp.float32) * scale
            terms = jnp.where(
                before, jnp.exp(scores - SOFTMAX_HEAT), jnp.where(eye, own, 0.0)
            )
            probs = terms * (1.0 / jnp.sum(terms, -1, keepdims=True))
            low = probs.astype(jnp.bfloat16)
            sbuf_att[head, rows] = jnp.dot(
                low, v_all, preferred_element_type=jnp.float32
            ).astype(jnp.bfloat16)
            dprob = lax.dot_general(g_b, v_all, nt, preferred_element_type=jnp.float32)
            delta = jnp.sum(probs * dprob, -1, keepdims=True)
            dscore = jnp.where(before, probs * (dprob - delta), 0.0).astype(jnp.bfloat16)
            qacc[rows, :] += jnp.dot(dscore, q_all, preferred_element_type=jnp.float32)
            qacc[pl.ds(0, upto), :] += lax.dot_general(
                dscore, q_b, tn, preferred_element_type=jnp.float32
            )
            vacc[pl.ds(0, upto), :] += lax.dot_general(
                low, g_b, tn, preferred_element_type=jnp.float32
            )
        dq = (qacc[...] * scale).astype(jnp.bfloat16).astype(jnp.float32)
        dy = inverse * dq - proj * inverse**3 * jnp.mean(dq * proj, -1, keepdims=True)
        ybuf[z, :, cols] = dy.astype(jnp.bfloat16)
        sbuf_vg[head] = vacc[...].astype(jnp.bfloat16)
        y_relay(0, head)
        place = pl.ds(pl.multiple_of(z * wide + head * HEAD_SIZE, HEAD_SIZE), HEAD_SIZE)
        att_ref[:, place] = sbuf_att[head, span(z, tok)]
        vg_ref[:, place] = sbuf_vg[head, span(z, tok)]

    for k in SHIFTS:
        h_copies[k].wait_recv()
    hturn[...] = jnp.transpose(hbuf[...])

    mid = depth // 2
    mine = pl.ds(pl.multiple_of(core * mid, mid), mid)
    other = pl.ds(pl.multiple_of((1 - core) * mid, mid), mid)
    core_copies, x_copies, last_copies = {}, {}, {}

    def add_chips(k):
        x_copies[k].wait_recv()
        at = span(origins[k], wide)
        total = both[k].astype(jnp.float32) + recv_x[k].astype(jnp.float32)
        wg_ref[mine, at] = total.astype(jnp.bfloat16)
        last_copies[k] = start(
            remote(
                wg_ref.at[mine, at], wg_ref.at[mine, at],
                rsend.at[2, k], rrecv.at[2, k], to_core,
            )
        )

    for k in range(n):
        if k > 0:
            for head in range(heads):
                y_relay(k, head)
        if k == 2:
            send_back(0)
        part[k] = jnp.dot(
            hturn[...], ybuf[origins[k]], preferred_element_type=jnp.float32
        ).astype(jnp.bfloat16)
        core_copies[k] = start(
            remote(part.at[k, other], recv_core.at[k], rsend.at[0, k], rrecv.at[0, k], to_core)
        )
        if k > 0:
            add_chips(k - 1)
        core_copies[k].wait_recv()
        both[k] = (
            part[k, mine, :].astype(jnp.float32) + recv_core[k].astype(jnp.float32)
        ).astype(jnp.bfloat16)
        x_copies[k] = start(
            remote(both.at[k], recv_x.at[k], rsend.at[1, k], rrecv.at[1, k], to_x)
        )

    send_back(1)
    own_rows = span(z, tok)
    for k in range(n):
        total = jnp.zeros((tok, depth), jnp.float32)
        for j in range(n):
            total = total + lax.dot_general(
                ybuf[origins[j], own_rows, :], wbuf[origins[k], :, span(origins[j], wide)], nt,
                preferred_element_type=jnp.float32,
            )
        hg_ref[:, span(origins[k], depth)] = total.astype(jnp.bfloat16)
    add_chips(n - 1)

    for k in SHIFTS:
        for head in range(heads):
            a_copies[k, head].wait_recv()
            d_copies[k, head].wait_recv()
    for k in range(n):
        last_copies[k].wait_recv()
    done = set(id(copy) for copy in p_copies.values())
    for copy in started:
        if id(copy) not in done:
            copy.wait_send()

    @pl.when(inner)
    def _():
        for copy in relayed:
            copy.wait_send()


def local_by_heads(hidden, shared_weight, values, clusters, cotangent):
    n = 4
    tok, model = hidden.shape[1:]
    depth, width = shared_weight.shape
    wide = width // n
    length = n * tok
    heads = wide // HEAD_SIZE
    ids = jnp.broadcast_to(clusters[0, :, 0].astype(jnp.float32)[None, :], (8, tok))
    bf, f32 = jnp.bfloat16, jnp.float32
    vm = pltpu.VMEM
    dma = pltpu.SemaphoreType.DMA
    scratch = [
        vm((tok, model), bf), vm((n, depth, width), bf), vm((length, wide), bf), vm((length, wide), bf),
        vm((length, wide), bf), vm((n, 8, tok), f32), vm((length, depth), bf),
        vm((n, length, wide), bf), vm((depth, length), bf), vm((length, HEAD_SIZE), f32),
        vm((length, HEAD_SIZE), f32), vm((tok, width), f32),
        vm((heads, length, HEAD_SIZE), bf), vm((heads, length, HEAD_SIZE), bf),
        vm((heads, length, HEAD_SIZE), bf), vm((n, depth, wide), bf),
        vm((n, depth // 2, wide), bf), vm((n, depth // 2, wide), bf), vm((n, depth // 2, wide), bf),
        dma((5,)), dma((2, n + 1)), dma((n, 2)), dma((3, n - 1, 2)), dma((3, n - 1, 2)),
    ]
    scratch += [dma((n - 1,)) for _ in range(10)]
    scratch += [dma((heads, n + 1)), dma((n, heads))]
    scratch += [dma((n - 1, heads)) for _ in range(4)]
    scratch += [dma((3, n)), dma((3, n))]
    att, hg, vg, wg = pl.pallas_call(
        along_heads_kernel,
        out_shape=(
            jax.ShapeDtypeStruct((tok, width), bf),
            jax.ShapeDtypeStruct((tok, model), bf),
            jax.ShapeDtypeStruct((tok, width), bf),
            jax.ShapeDtypeStruct((depth, width), bf),
        ),
        in_specs=[pl.BlockSpec(memory_space=pl.ANY)] * 4
        + [pl.BlockSpec(memory_space=pltpu.VMEM)],
        out_specs=[pl.BlockSpec(memory_space=pltpu.VMEM)] * 4,
        scratch_shapes=scratch,
        compiler_params=pltpu.CompilerParams(
            collective_id=0, has_side_effects=True, vmem_limit_bytes=48 * 1024 * 1024
        ),
        cost_estimate=pl.CostEstimate(
            flops=8 * tok * model * width, bytes_accessed=8 * 1024 * 1024, transcendentals=length * length
        ),
    )(hidden[0], shared_weight, values[0], cotangent[0], ids)
    return att[None], hg[None], vg[None], wg.astype(f32)


def solution(mesh):
    placed = (
        P(("groups", "rep"), "seq", None),
        P("seq", None),
        P(("groups", "rep"), "seq", None),
        P(("groups", "rep"), "seq", None),
        P(("groups", "rep"), "seq", None),
    )
    by_heads = (mesh.shape["groups"], mesh.shape["seq"], mesh.shape["rep"]) == (2, 4, 4)
    return jax.shard_map(
        local_by_heads if by_heads else local,
        mesh=mesh,
        in_specs=placed,
        out_specs=(
            P(("groups", "rep"), "seq", None),
            P(("groups", "rep"), "seq", None),
            P(("groups", "rep"), "seq", None),
            P(("groups", "seq"), None),
        ),
        check_vma=False,
    )
```
